32 devices in a mesh: chan: 8 (over z, y), win: 4 (over x, core).
Axes of the slice: x: 2, y: 2, z: 4, core: 2. Of those that a mesh axis runs over, the one named last changes fastest.
Arguments:
- spectra: bfloat16 [384, 16, 2, 1024], P('chan', 'win'), may hold values from -120 to 120
- sources: int32 [4], replicated, may hold values from 0 to 383
- bin_rows: int32 [4, 8, 32, 3], P(None, 'chan'), may hold values from -1 to 47, as said below
Outputs:
- stacked: float32 [4, 32, 4096], P(None, 'chan', 'win')
The draws below stay inside these ranges and needn't reach their ends.
Inputs may be any that keep to these rules, and one draw needn't show every extreme that they name: `bin_rows`: for every step and every index d of chan, the entries name each of that device's 48 local receiver rows exactly once; within a bin the used slots come first and the rest are -1. In each step one bin uses all 3 slots on every device.
All inputs are finite; a program needn't handle non-finite values.
Results may differ from the reference program's by a relative error of at most 0.0099.
Values may be sent and summed in bfloat16 or wider, within the bound.
A program may use at most 768 MiB of HBM per device.

```python
import math
import jax
import jax.numpy as jnp
from jax import lax

CH_DEV = 48
STEPS = 4
F = 1024
F0 = 32
NFFT = 8192
LMAX = 2048
HW = 32
NBINS = 32
MOST = 3
LAGS = 4096
CHANNELS = 384
WINDOWS = 16
N_CHAN = 8


def draw_spectra(key, part):
    first_key, second_key, third_key = jax.random.split(jax.random.fold_in(key, 5), 3)
    full_shape = (CHANNELS, WINDOWS, 2, F)
    base_noise = jnp.clip(jax.random.normal(first_key, full_shape, jnp.float32), -6.0, 6.0)
    channel_scale = jnp.exp(jax.random.uniform(second_key, (CHANNELS, WINDOWS, 1, 1), jnp.float32, 0.0, math.log(10.0)))
    band_scale = jnp.exp(jax.random.uniform(third_key, (CHANNELS, 1, 1, F), jnp.float32, math.log(0.5), math.log(2.0)))
    return (base_noise * channel_scale * band_scale).astype(jnp.bfloat16)


def draw_bin_rows(key, part):
    step_keys = jax.random.split(jax.random.fold_in(key, 11), STEPS)

    def one_step(step_key):
        weight_key, forced_key, device_key = jax.random.split(step_key, 3)
        weight = jax.random.randint(weight_key, (NBINS,), 0, 4)
        forced = jax.random.randint(forced_key, (), 0, NBINS)
        device_keys = jax.random.split(device_key, N_CHAN)

        def one_device(single_key):
            jitter_key, order_key = jax.random.split(single_key)
            jitter = jax.random.randint(jitter_key, (NBINS, MOST), 0, 1 << 14)
            bin_index = jnp.arange(NBINS, dtype=jnp.int32)
            scores = jitter + weight[:, None] * (1 << 12) + jnp.where(bin_index == forced, 1 << 16, 0)[:, None]
            flat_scores = scores.reshape(-1) * (NBINS * MOST) + jnp.arange(NBINS * MOST, dtype=jnp.int32)
            _, chosen = lax.top_k(flat_scores, CH_DEV)
            picked = jnp.zeros((NBINS * MOST,), jnp.int32).at[chosen].set(1).reshape(NBINS, MOST)
            counts = jnp.sum(picked, axis=1)
            filled = (jnp.arange(MOST, dtype=jnp.int32)[None, :] < counts[:, None]).astype(jnp.int32).reshape(-1)
            fill_rank = jnp.cumsum(filled) - 1
            row_order = jax.random.permutation(order_key, CH_DEV).astype(jnp.int32)
            entries = jnp.where(filled > 0, row_order[jnp.clip(fill_rank, 0, CH_DEV - 1)], -1)
            return entries.reshape(NBINS, MOST).astype(jnp.int32)
        return jax.vmap(one_device)(device_keys)
    return jax.vmap(one_step)(step_keys)


def touch_ends(values, own_key, smallest, largest):
    dims = values.shape
    index_at = [jax.random.randint(jax.random.fold_in(own_key, axis), (), 0, dims[axis]) for axis in range(len(dims))]
    values = values.at[tuple(index_at)].set(smallest)
    longest = dims.index(max(dims))
    index_at[longest] = (index_at[longest] + 1) % dims[longest]
    return values.at[tuple(index_at)].set(largest)


def setup_inputs(seed: int = 0) -> dict:
    keys = jax.random.split(jax.random.key(seed), 4)
    return {
        "spectra": draw_spectra(jax.random.fold_in(keys[3], 71), 0),
        "sources": touch_ends(jax.random.randint(keys[1], (STEPS,), 0, CHANNELS), jax.random.fold_in(keys[1], 1), 0, CHANNELS - 1).astype(jnp.int32),
        "bin_rows": draw_bin_rows(jax.random.fold_in(keys[3], 71), 0),
    }


epsilon_amp = 1e-06
phase_floor = 0.1

def band_matrix():
    index = jnp.arange(F, dtype=jnp.int32)
    inside = jnp.abs(index[:, None] - index[None, :]) <= HW
    return inside.astype(jnp.float32) / (2 * HW + 1)

def whiten(spectra):
    real_part = spectra[:, :, 0, :].astype(jnp.float32)
    imag_part = spectra[:, :, 1, :].astype(jnp.float32)
    amplitude = jnp.sqrt(real_part * real_part + imag_part * imag_part)
    smooth = jnp.dot(amplitude.reshape(-1, F), band_matrix(), precision=lax.Precision.HIGHEST)
    smooth = smooth.reshape(amplitude.shape) + epsilon_amp
    return jnp.stack([real_part / smooth, imag_part / smooth], axis=2).astype(jnp.bfloat16)

def cross_spectra(white, source):
    white_real = white[..., 0, :].astype(jnp.float32)
    white_imag = white[..., 1, :].astype(jnp.float32)
    source_real = source[..., 0, :].astype(jnp.float32)
    source_imag = source[..., 1, :].astype(jnp.float32)
    cross_real = white_real * source_real + white_imag * source_imag
    cross_imag = white_imag * source_real - white_real * source_imag
    return jnp.concatenate([cross_real, cross_imag], axis=-1).astype(jnp.bfloat16)

def lag_table(first_lag, lag_count):
    frequency = F0 + jnp.arange(F, dtype=jnp.int32)
    lag_index = first_lag + jnp.arange(lag_count, dtype=jnp.int32) - LMAX
    turn_count = jnp.mod(frequency[:, None] * lag_index[None, :], NFFT)
    angle_rad = turn_count.astype(jnp.float32) * (2.0 * jnp.pi / NFFT)
    cosine = jnp.cos(angle_rad)
    sine_part = jnp.sin(angle_rad)
    upper_half = jnp.concatenate([cosine, sine_part], axis=1)
    lower_half = jnp.concatenate([-sine_part, cosine], axis=1)
    return jnp.concatenate([upper_half, lower_half], axis=0).astype(jnp.bfloat16)

def correlate_block(cross_rows, first_lag, lag_count, windows):
    analytic = jnp.dot(cross_rows, lag_table(first_lag, lag_count), preferred_element_type=jnp.float32)
    analytic = analytic * (1.0 / jnp.sqrt(jnp.float32(F)))
    real_part = analytic[:, :lag_count]
    imag_part = analytic[:, lag_count:]
    magnitude = jnp.maximum(jnp.sqrt(real_part * real_part + imag_part * imag_part), phase_floor)
    terms = jnp.stack([real_part, real_part / magnitude, imag_part / magnitude], axis=1)
    return terms.reshape(-1, windows, 3, lag_count).sum(axis=1)

def weigh_stack(totals, counts, windows):
    traces = jnp.maximum(counts, 1.0) * windows
    linear = totals[..., 0, :]
    power = totals[..., 1, :] * totals[..., 1, :] + totals[..., 2, :] * totals[..., 2, :]
    return linear / jnp.sqrt(traces)[..., None] * power / traces[..., None]

def reference(spectra, sources, bin_rows):
    white = whiten(spectra)
    block_len = min(256, LAGS)
    block_count = LAGS // block_len
    device_base = jnp.arange(N_CHAN, dtype=jnp.int32)[:, None, None] * CH_DEV
    channel_index = jnp.arange(CHANNELS, dtype=jnp.int32)
    results = []
    for step_index in range(STEPS):
        source = lax.dynamic_index_in_dim(white, sources[step_index], 0, keepdims=False)
        cross_rows = cross_spectra(white, source).reshape(-1, 2 * F)
        slot_rows = bin_rows[step_index]
        is_live = slot_rows >= 0
        channel_ids = device_base + slot_rows
        member = lax.optimization_barrier(jnp.sum(((channel_ids[..., None] == channel_index) & is_live[..., None]).astype(jnp.float32), axis=(0, 2)))
        counts = lax.optimization_barrier(jnp.sum(member, axis=1))

        def one_block(block):
            partial_value = correlate_block(cross_rows, block * block_len, block_len, WINDOWS)
            return jnp.einsum('bc,ctl->btl', member, partial_value, precision=lax.Precision.HIGHEST)
        pieces = lax.map(one_block, jnp.arange(block_count, dtype=jnp.int32))
        totals = jnp.transpose(pieces, (1, 2, 0, 3)).reshape(NBINS, 3, LAGS)
        results.append(weigh_stack(totals, counts, WINDOWS))
    return jnp.stack(results)
```

```python
import functools

import jax
import jax.numpy as jnp
import ml_dtypes
import numpy as np
from jax import lax
from jax.experimental import pallas as pl
from jax.experimental.pallas import tpu as pltpu
from jax.sharding import PartitionSpec as P

F = 1024
F0 = 32
NFFT = 8192
LMAX = 2048
HW = 32
NBINS = 32
MOST = 3
LAGS = 4096
CHUNK = 256

epsilon_amp = 1e-06
phase_floor = 0.1

f32 = jnp.float32
bf16 = jnp.bfloat16
MESH = pl.DeviceIdType.MESH


def lag_tables(lag_dev):
    blocks = LMAX // lag_dev
    units = lag_dev // CHUNK
    freq = F0 + np.arange(F, dtype=np.int64)

    def trig(lags):
        turn = (freq[:, None] * lags[None, :]) % NFFT
        angle = turn * (2.0 * np.pi / NFFT)
        scale = F ** -0.5
        return np.cos(angle).astype(ml_dtypes.bfloat16), np.sin(angle).astype(ml_dtypes.bfloat16), scale

    table = np.zeros((units, blocks, F, 2 * CHUNK), ml_dtypes.bfloat16)
    for u in range(units):
        for m in range(blocks):
            cosine, sine, scale = trig(m * lag_dev + u * CHUNK + np.arange(CHUNK))
            both = np.concatenate([cosine, sine], axis=1).astype(np.float32) * scale
            table[u, m] = both.astype(ml_dtypes.bfloat16)
    edge = np.zeros((F, 256), np.float32)
    cosine, sine, scale = trig((np.arange(blocks) + 1) * lag_dev)
    edge[:, :blocks] = cosine.astype(np.float32) * scale
    edge[:, 128 : 128 + blocks] = sine.astype(np.float32) * scale
    return table, edge.astype(ml_dtypes.bfloat16)


def dot(a, b):
    return jnp.dot(a, b, preferred_element_type=f32)


def smooth_band(amp, band):
    hi = amp.astype(bf16)
    lo = (amp - hi.astype(f32)).astype(bf16)
    count = F // 256
    parts = []
    for j in range(count):
        first, last = max(j - 1, 0), min(j + 2, count)
        piece = band[(first - j + 1) * 256 : (last - j + 1) * 256, :]
        cols = slice(first * 256, last * 256)
        parts.append(dot(hi[:, cols], piece) + dot(lo[:, cols], piece))
    return jnp.concatenate(parts, axis=1) * (1.0 / (2 * HW + 1)) + epsilon_amp


def whiten(re, im, band):
    inv = 1.0 / smooth_band(jnp.sqrt(re * re + im * im), band)
    return (re * inv).astype(bf16), (im * inv).astype(bf16)


def kernel(
    cfg,
    x_ref, srccol_ref, kcol_ref, cnt_ref, edge_ref, tab_hbm,
    o_ref,
    tab, sbuf, rsr, ag, wr_s, wi_s, sr_s, si_s, xs, wmat, ts, oe, traces,
    p1, r1, a2, b2, r2, a3, b3, r3, a4, b4, r4,
    tab_sem, rs_s, rs_r, ag_s, ag_r, s1, q1, s2, q2, s3, q3, s4, q4,
):
    nchan, nwin, steps, wd, chd, units, blocks = cfg
    g2, g4 = nwin // 2, nchan // 2
    rows = wd * chd
    me_c, me_w = lax.axis_index("chan"), lax.axis_index("win")
    w1, w2 = lax.rem(me_w, 2), me_w // 2
    c1, c2 = lax.rem(me_c, 2), me_c // 2

    def chan_dev(k):
        return (lax.rem(me_c + k, nchan), me_w)

    def dev1():
        return (me_c, me_w + 1 - 2 * w1)

    def dev2(k):
        return (me_c, lax.rem(w2 + k, g2) * 2 + w1)

    def dev3():
        return (me_c + 1 - 2 * c1, me_w)

    def dev4(k):
        return (lax.rem(c2 + k, g4) * 2 + c1, me_w)

    def table_copy(u):
        return pltpu.make_async_copy(tab_hbm.at[u], tab.at[u], tab_sem.at[u])

    def remote(src, dst, s, r, dev):
        return pltpu.make_async_remote_copy(
            src_ref=src, dst_ref=dst, send_sem=s, recv_sem=r, device_id=dev, device_id_type=MESH
        )

    for u in range(units):
        table_copy(u).start()

    barrier = pltpu.get_barrier_semaphore()
    partners = [chan_dev(k) for k in range(1, nchan)] + [dev1()] + [dev2(k) for k in range(1, g2)]
    for dev in partners:
        pl.semaphore_signal(barrier, inc=1, device_id=dev, device_id_type=MESH)

    piece = 2 * F // nchan
    col = lax.broadcasted_iota(jnp.int32, (steps * wd, rows), 1)
    pick = jnp.where(col == srccol_ref[...], 1.0, 0.0).astype(bf16)
    both = jnp.concatenate([dot(pick, x_ref[0]), dot(pick, x_ref[1])], axis=1).astype(bf16)
    for d in range(nchan):
        sbuf[d, :, :piece] = both[:, d * piece : (d + 1) * piece]
        sbuf[d, :, piece:] = cnt_ref[d]
    pl.semaphore_wait(barrier, len(partners))

    def rs_copy(k):
        return remote(
            sbuf.at[lax.rem(me_c + k, nchan)], rsr.at[k - 1], rs_s.at[k - 1], rs_r.at[k - 1], chan_dev(k)
        )

    def ag_copy(k):
        return remote(ag.at[me_c], ag.at[me_c], ag_s.at[k - 1], ag_r.at[k - 1], chan_dev(k))

    for k in range(1, nchan):
        rs_copy(k).start()

    kc = kcol_ref[...]
    wcol = lax.broadcasted_iota(jnp.int32, wmat.shape, 1)
    hit = (wcol == kc[:, 0:1]) | (wcol == kc[:, 1:2]) | (wcol == kc[:, 2:3])
    wmat[...] = jnp.where(hit, 1.0, 0.0).astype(bf16)
    bi = lax.broadcasted_iota(jnp.int32, (768, 256), 0)
    bj = lax.broadcasted_iota(jnp.int32, (768, 256), 1)
    band = jnp.where(jnp.abs(bi - 256 - bj) <= HW, 1.0, 0.0).astype(bf16)

    for k in range(1, nchan):
        rs_copy(k).wait()
    total = sbuf[me_c].astype(f32)
    for k in range(1, nchan):
        total = total + rsr[k - 1].astype(f32)
    ag[me_c] = total[:, :piece].astype(bf16)
    traces[...] = jnp.maximum(total[:, piece:], 1.0) * (wd * nwin)
    for k in range(1, nchan):
        ag_copy(k).start()

    wr, wi = whiten(x_ref[0].astype(f32), x_ref[1].astype(f32), band)
    wr_s[...] = wr
    wi_s[...] = wi

    for k in range(1, nchan):
        ag_copy(k).wait()
    half = nchan // 2
    sre = jnp.concatenate([ag[d] for d in range(half)], axis=1).astype(f32)
    sim = jnp.concatenate([ag[d] for d in range(half, nchan)], axis=1).astype(f32)
    sr, si = whiten(sre, sim, band)
    sr_s[...] = sr.astype(f32)
    si_s[...] = si.astype(f32)

    for w in range(wd):
        here = slice(w * chd, (w + 1) * chd)
        wrw = wr_s[here, :].astype(f32)
        wiw = wi_s[here, :].astype(f32)
        for s in range(steps):
            i = s * wd + w
            a, b = sr_s[i : i + 1, :], si_s[i : i + 1, :]
            xs[s, here, :] = (wrw * a + wiw * b).astype(bf16)
            xs[s, slice(rows + w * chd, rows + (w + 1) * chd), :] = (wiw * a - wrw * b).astype(bf16)

    def add_terms(sign, s, re, im, lanes):
        inv = lax.rsqrt(jnp.maximum(re * re + im * im, phase_floor * phase_floor))
        for q, value in enumerate((re, re * inv, im * inv)):
            total = value[:chd]
            for w in range(1, wd):
                total = total + value[w * chd : (w + 1) * chd]
            first = (s * 3 + q) * chd
            ts[sign, first : first + chd, :lanes] = total.astype(bf16)

    for s in range(steps):
        res = dot(xs[s], edge_ref[...])
        add_terms(1, s, res[:rows, :128] + res[rows:, 128:], res[rows:, :128] - res[:rows, 128:], 128)
    oe[...] = dot(wmat[...], ts[1, :, :128])

    def compute(u, m):
        for s in range(steps):
            res = dot(xs[s], tab[u, m])
            a, c = res[:rows, :CHUNK], res[:rows, CHUNK:]
            d, b = res[rows:, :CHUNK], res[rows:, CHUNK:]
            add_terms(0, s, a - b, c + d, CHUNK)
            add_terms(1, s, a + b, d - c, CHUNK)
        pos = blocks + m
        neg = blocks - 1 - m
        part = p1.shape[3:]
        p1[u, pos % 2, pos // 2] = dot(wmat[...], ts[0]).reshape(part)
        lane = lax.broadcasted_iota(jnp.int32, (wmat.shape[0], CHUNK), 1)
        value = dot(wmat[...], ts[1])
        value = jnp.where((lane + u) == 0, oe[:, m : m + 1], value)
        p1[u, neg % 2, neg // 2] = value.reshape(part)

    def copy1(u):
        return remote(p1.at[u, 1 - w1], r1.at[u], s1.at[u], q1.at[u], dev1())

    def copy2(u, k):
        return remote(
            b2.at[u, lax.rem(w2 + k, g2)], r2.at[u, k - 1], s2.at[u, k - 1], q2.at[u, k - 1], dev2(k)
        )

    def copy3(u):
        return remote(b3.at[u, 1 - c1], r3.at[u], s3.at[u], q3.at[u], dev3())

    def copy4(u, k):
        return remote(
            b4.at[u, lax.rem(c2 + k, g4)], r4.at[u, k - 1], s4.at[u, k - 1], q4.at[u, k - 1], dev4(k)
        )

    def stage2(u):
        copy1(u).wait()
        for i in range(g2):
            b2[u, i] = (p1[u, w1, i] + r1[u, i]).astype(bf16)
        for k in range(1, g2):
            copy2(u, k).start()
        a2[u] = p1[u, w1, w2] + r1[u, w2]

    def stage3(u):
        for k in range(1, g2):
            copy2(u, k).wait()
        for i in range(2):
            total = a2[u, i]
            for k in range(1, g2):
                total = total + r2[u, k - 1, i].astype(f32)
            a3[u, i] = total
            b3[u, i] = total.astype(bf16)
        copy3(u).start()

    def stage4(u):
        copy3(u).wait()
        for i in range(g4):
            total = a3[u, c1, i] + r3[u, i].astype(f32)
            a4[u, i] = total
            b4[u, i] = total.astype(bf16)
        for k in range(1, g4):
            copy4(u, k).start()

    def stage5(u):
        for k in range(1, g4):
            copy4(u, k).wait()
        total = a4[u, c2]
        for k in range(1, g4):
            total = total + r4[u, k - 1].astype(f32)
        n = total.shape[0] // 3
        lin, pr, pi = total[:n], total[n : 2 * n], total[2 * n :]
        count = traces[:n, 0:1]
        o_ref[u] = lin * lax.rsqrt(count) * ((pr * pr + pi * pi) / count)

    def turn(v, carry):
        @pl.when(v < units)
        def _():
            table_copy(v).wait()
            compute(v, 0)

        @pl.when((v >= 1) & (v < units + 1))
        def _():
            stage2(v - 1)

        @pl.when((v >= 2) & (v < units + 2))
        def _():
            stage3(v - 2)

        @pl.when((v >= 3) & (v < units + 3))
        def _():
            stage4(v - 3)

        @pl.when(v >= 4)
        def _():
            stage5(v - 4)

        @pl.when(v < units)
        def _():
            for m in range(1, blocks):
                compute(v, m)
            copy1(v).start()

        return carry

    lax.fori_loop(0, units + 4, turn, 0)


def shards(spectra, sources, bin_rows):
    chd, wd = spectra.shape[0], spectra.shape[1]
    steps = sources.shape[0]
    nchan, nwin = lax.axis_size("chan"), lax.axis_size("win")
    lag_dev = LAGS // nwin
    units, blocks = lag_dev // CHUNK, nwin // 2
    bl = NBINS // nchan
    rows = wd * chd
    g2, g4 = nwin // 2, nchan // 2
    me = lax.axis_index("chan")

    x = jnp.transpose(spectra, (2, 1, 0, 3)).reshape(2, rows, F)
    loc = sources - me * chd
    ok = (loc >= 0) & (loc < chd)
    srccol = jnp.where(ok[:, None], loc[:, None] + jnp.arange(wd, dtype=jnp.int32)[None] * chd, -1)
    srccol = srccol.reshape(steps * wd, 1)

    slots = bin_rows[:, 0].reshape(steps, g4, 2, bl, MOST)
    slots = jnp.transpose(slots, (2, 1, 0, 3, 4))[:, :, None]
    step_at = jnp.arange(steps, dtype=jnp.int32)[:, None, None] * (3 * chd)
    term_at = jnp.arange(3, dtype=jnp.int32)[:, None, None, None] * chd
    kcol = jnp.where(slots >= 0, slots + step_at + term_at, -1).reshape(NBINS * 3 * steps, MOST)
    live = jnp.sum((bin_rows[:, 0] >= 0).astype(f32), axis=-1).reshape(steps, nchan, bl)
    live = jnp.transpose(live, (1, 0, 2)).reshape(nchan, steps * bl, 1)
    live = jnp.pad(live, ((0, 0), (0, steps * wd - steps * bl), (0, 0)))
    cnt = jnp.broadcast_to(live, (nchan, steps * wd, 128)).astype(bf16)

    table, edge = lag_tables(lag_dev)
    per = NBINS * 3 * steps // nchan
    piece = 2 * F // nchan
    tail = (per, CHUNK)
    cfg = (nchan, nwin, steps, wd, chd, units, blocks)
    dma = pltpu.SemaphoreType.DMA
    vmem = pl.BlockSpec(memory_space=pltpu.VMEM)
    out = pl.pallas_call(
        functools.partial(kernel, cfg),
        out_shape=jax.ShapeDtypeStruct((units, steps * bl, CHUNK), f32),
        in_specs=[vmem] * 5 + [pl.BlockSpec(memory_space=pl.ANY)],
        out_specs=vmem,
        scratch_shapes=[
            pltpu.VMEM((units, blocks, F, 2 * CHUNK), bf16),
            pltpu.VMEM((nchan, steps * wd, piece + 128), bf16),
            pltpu.VMEM((nchan - 1, steps * wd, piece + 128), bf16),
            pltpu.VMEM((nchan, steps * wd, piece), bf16),
            pltpu.VMEM((rows, F), bf16),
            pltpu.VMEM((rows, F), bf16),
            pltpu.VMEM((steps * wd, F), f32),
            pltpu.VMEM((steps * wd, F), f32),
            pltpu.VMEM((steps, 2 * rows, F), bf16),
            pltpu.VMEM((NBINS * 3 * steps, 3 * steps * chd), bf16),
            pltpu.VMEM((2, 3 * steps * chd, CHUNK), bf16),
            pltpu.VMEM((NBINS * 3 * steps, 128), f32),
            pltpu.VMEM((steps * wd, 128), f32),
            pltpu.VMEM((units, 2, g2, 2, g4) + tail, f32),
            pltpu.VMEM((units, g2, 2, g4) + tail, f32),
            pltpu.VMEM((units, 2, g4) + tail, f32),
            pltpu.VMEM((units, g2, 2, g4) + tail, bf16),
            pltpu.VMEM((units, g2 - 1, 2, g4) + tail, bf16),
            pltpu.VMEM((units, 2, g4) + tail, f32),
            pltpu.VMEM((units, 2, g4) + tail, bf16),
            pltpu.VMEM((units, g4) + tail, bf16),
            pltpu.VMEM((units, g4) + tail, f32),
            pltpu.VMEM((units, g4) + tail, bf16),
            pltpu.VMEM((units, g4 - 1) + tail, bf16),
            dma((units,)),
            dma((nchan - 1,)), dma((nchan - 1,)), dma((nchan - 1,)), dma((nchan - 1,)),
            dma((units,)), dma((units,)),
            dma((units, g2 - 1)), dma((units, g2 - 1)),
            dma((units,)), dma((units,)),
            dma((units, g4 - 1)), dma((units, g4 - 1)),
        ],
        compiler_params=pltpu.CompilerParams(
            collective_id=0, has_side_effects=True, vmem_limit_bytes=56 * 1024 * 1024
        ),
        name="stack",
    )(x, srccol, kcol, cnt, jnp.asarray(edge), jnp.asarray(table))
    out = jnp.transpose(out, (1, 0, 2)).reshape(steps, bl, lag_dev)
    mirrored = jnp.roll(jnp.flip(out, axis=-1), 1, axis=-1)
    return jnp.where(lax.axis_index("win") < blocks, mirrored, out)


def solution(mesh):
    in_specs = (P("chan", "win", None, None), P(), P(None, "chan", None, None))
    out_specs = P(None, "chan", "win")
    return jax.shard_map(shards, mesh=mesh, in_specs=in_specs, out_specs=out_specs, check_vma=False)
```

```python
import functools

import jax
import jax.numpy as jnp
import ml_dtypes
import numpy as np
from jax import lax
from jax.experimental import pallas as pl
from jax.experimental.pallas import tpu as pltpu
from jax.sharding import PartitionSpec as P

F = 1024
F0 = 32
NFFT = 8192
LMAX = 2048
HW = 32
NBINS = 32
MOST = 3
LAGS = 4096
CHUNK = 128

epsilon_amp = 1e-06
phase_floor = 0.1

f32 = jnp.float32
bf16 = jnp.bfloat16
MESH = pl.DeviceIdType.MESH


def lag_tables(lag_dev):
    blocks = LMAX // lag_dev
    units = lag_dev // CHUNK
    freq = F0 + np.arange(F, dtype=np.int64)

    def trig(lags):
        turn = (freq[:, None] * lags[None, :]) % NFFT
        angle = turn * (2.0 * np.pi / NFFT)
        scale = F ** -0.5
        return np.cos(angle).astype(ml_dtypes.bfloat16), np.sin(angle).astype(ml_dtypes.bfloat16), scale

    table = np.zeros((units, blocks, F, 2 * CHUNK), ml_dtypes.bfloat16)
    for u in range(units):
        for m in range(blocks):
            cosine, sine, scale = trig(m * lag_dev + u * CHUNK + np.arange(CHUNK))
            both = np.concatenate([cosine, sine], axis=1).astype(np.float32) * scale
            table[u, m] = both.astype(ml_dtypes.bfloat16)
    edge = np.zeros((F, 256), np.float32)
    cosine, sine, scale = trig((np.arange(blocks) + 1) * lag_dev)
    edge[:, :blocks] = cosine.astype(np.float32) * scale
    edge[:, 128 : 128 + blocks] = sine.astype(np.float32) * scale
    return table, edge.astype(ml_dtypes.bfloat16)


def dot(a, b):
    return jnp.dot(a, b, preferred_element_type=f32)


def smooth_band(amp, band):
    hi = amp.astype(bf16)
    lo = (amp - hi.astype(f32)).astype(bf16)
    count = F // 256
    parts = []
    for j in range(count):
        first, last = max(j - 1, 0), min(j + 2, count)
        piece = band[(first - j + 1) * 256 : (last - j + 1) * 256, :]
        cols = slice(first * 256, last * 256)
        parts.append(dot(hi[:, cols], piece) + dot(lo[:, cols], piece))
    return jnp.concatenate(parts, axis=1) * (1.0 / (2 * HW + 1)) + epsilon_amp


def whiten(re, im, band):
    inv = 1.0 / smooth_band(jnp.sqrt(re * re + im * im), band)
    return (re * inv).astype(bf16), (im * inv).astype(bf16)


def kernel(
    cfg,
    x_ref, sources_ref, bins_ref, edge_ref, tab_hbm,
    o_ref,
    tab, sbuf, rsr, ag, wr_s, wi_s, sr_s, si_s, xs, wmat, ts, oe, traces, fin,
    p1, r1, a2, b2, r2, a3, b3, r3, a4, b4, r4,
    tab_sem, rs_s, rs_r, ag_s, ag_r, s1, q1, s2, q2, s3, q3, s4, q4,
):
    nchan, nwin, steps, wd, chd, units, blocks = cfg
    g2, g4 = nwin // 2, nchan // 2
    rows = wd * chd
    me_c, me_w = lax.axis_index("chan"), lax.axis_index("win")
    w1, w2 = lax.rem(me_w, 2), me_w // 2
    c1, c2 = lax.rem(me_c, 2), me_c // 2

    def chan_dev(k):
        return (lax.rem(me_c + k, nchan), me_w)

    def dev1():
        return (me_c, me_w + 1 - 2 * w1)

    def dev2(k):
        return (me_c, lax.rem(w2 + k, g2) * 2 + w1)

    def dev3():
        return (me_c + 1 - 2 * c1, me_w)

    def dev4(k):
        return (lax.rem(c2 + k, g4) * 2 + c1, me_w)

    def table_copy(u):
        return pltpu.make_async_copy(tab_hbm.at[u], tab.at[u], tab_sem.at[u])

    def remote(src, dst, s, r, dev):
        return pltpu.make_async_remote_copy(
            src_ref=src, dst_ref=dst, send_sem=s, recv_sem=r, device_id=dev, device_id_type=MESH
        )

    for u in range(units):
        table_copy(u).start()

    barrier = pltpu.get_barrier_semaphore()
    partners = [chan_dev(k) for k in range(1, nchan)] + [dev1()] + [dev2(k) for k in range(1, g2)]
    for dev in partners:
        pl.semaphore_signal(barrier, inc=1, device_id=dev, device_id_type=MESH)

    piece = 2 * F // nchan
    bl = NBINS // nchan
    row = lax.broadcasted_iota(jnp.int32, (steps * wd, rows), 0)
    col = lax.broadcasted_iota(jnp.int32, (steps * wd, rows), 1)
    want = jnp.full(row.shape, -1, jnp.int32)
    for s in range(steps):
        loc = sources_ref[s] - me_c * chd
        loc = jnp.where((loc >= 0) & (loc < chd), loc, -wd * chd - 1)
        want = jnp.where(row // wd == s, (row % wd) * chd + loc, want)
    pick = jnp.where(col == want, 1.0, 0.0).astype(bf16)
    both = jnp.concatenate([dot(pick, x_ref[0]), dot(pick, x_ref[1])], axis=1).astype(bf16)
    slots = bins_ref[...].reshape(steps * NBINS, MOST)
    live = jnp.sum(jnp.where(slots >= 0, 1.0, 0.0), axis=1, keepdims=True)
    live = jnp.broadcast_to(live, (steps * NBINS, 128)).astype(bf16)

    def row_of(shape, dims):
        i = lax.broadcasted_iota(jnp.int32, shape, len(shape) - 2)
        b = sum(lax.broadcasted_iota(jnp.int32, shape, d) * size for d, size in dims)
        here = (i // bl) * NBINS + b * bl + i % bl
        hit = lax.broadcasted_iota(jnp.int32, shape, len(shape) - 1) == here
        return jnp.where(hit, 1.0, 0.0), i // bl

    shape = (nchan, steps * bl, steps * NBINS)
    chosen, _ = row_of(shape, [(0, 1)])
    cnt = dot(chosen.reshape(nchan * steps * bl, steps * NBINS).astype(bf16), live).astype(bf16)
    for d in range(nchan):
        sbuf[d, :, :piece] = both[:, d * piece : (d + 1) * piece]
        sbuf[d, :, piece:] = jnp.zeros((steps * wd, 128), bf16)
        sbuf[d, : steps * bl, piece:] = cnt[d * steps * bl : (d + 1) * steps * bl]
    pl.semaphore_wait(barrier, len(partners))

    def rs_copy(k):
        return remote(
            sbuf.at[lax.rem(me_c + k, nchan)], rsr.at[k - 1], rs_s.at[k - 1], rs_r.at[k - 1], chan_dev(k)
        )

    def ag_copy(k):
        return remote(ag.at[me_c], ag.at[me_c], ag_s.at[k - 1], ag_r.at[k - 1], chan_dev(k))

    for k in range(1, nchan):
        rs_copy(k).start()

    bi = lax.broadcasted_iota(jnp.int32, (768, 256), 0)
    bj = lax.broadcasted_iota(jnp.int32, (768, 256), 1)
    band = jnp.where(jnp.abs(bi - 256 - bj) <= HW, 1.0, 0.0).astype(bf16)
    wr, wi = whiten(x_ref[0].astype(f32), x_ref[1].astype(f32), band)
    wr_s[...] = wr
    wi_s[...] = wi

    for k in range(1, nchan):
        rs_copy(k).wait()
    total = sbuf[me_c].astype(f32)
    for k in range(1, nchan):
        total = total + rsr[k - 1].astype(f32)
    ag[me_c] = total[:, :piece].astype(bf16)
    traces[...] = jnp.maximum(total[:, piece:], 1.0) * (wd * nwin)
    for k in range(1, nchan):
        ag_copy(k).start()

    shape = (2, g4, 3, steps * bl, steps * NBINS)
    chosen, step = row_of(shape, [(0, 1), (1, 2)])
    chosen = chosen.reshape(-1, steps * NBINS).astype(bf16)
    offset = (step * 3 + lax.broadcasted_iota(jnp.int32, shape, 2)).astype(f32) * chd
    offset = offset.reshape(-1, steps * NBINS)[:, 0:1]
    slots_at = dot(chosen, slots.astype(f32).astype(bf16))
    slots_at = jnp.where(slots_at >= 0.0, slots_at + offset, -1.0)
    wcol = lax.broadcasted_iota(jnp.int32, wmat.shape, 1).astype(f32)
    hit = wcol == slots_at[:, 0:1]
    for k in range(1, MOST):
        hit = hit | (wcol == slots_at[:, k : k + 1])
    wmat[...] = jnp.where(hit, 1.0, 0.0).astype(bf16)

    for k in range(1, nchan):
        ag_copy(k).wait()
    half = nchan // 2
    sre = jnp.concatenate([ag[d] for d in range(half)], axis=1).astype(f32)
    sim = jnp.concatenate([ag[d] for d in range(half, nchan)], axis=1).astype(f32)
    sr, si = whiten(sre, sim, band)
    sr_s[...] = sr.astype(f32)
    si_s[...] = si.astype(f32)

    for w in range(wd):
        here = slice(w * chd, (w + 1) * chd)
        wrw = wr_s[here, :].astype(f32)
        wiw = wi_s[here, :].astype(f32)
        for s in range(steps):
            i = s * wd + w
            a, b = sr_s[i : i + 1, :], si_s[i : i + 1, :]
            xs[s, here, :] = (wrw * a + wiw * b).astype(bf16)
            xs[s, slice(rows + w * chd, rows + (w + 1) * chd), :] = (wiw * a - wrw * b).astype(bf16)

    def add_terms(sign, s, re, im):
        inv = lax.rsqrt(jnp.maximum(re * re + im * im, phase_floor * phase_floor))
        for q, value in enumerate((re, re * inv, im * inv)):
            total = value[:chd]
            for w in range(1, wd):
                total = total + value[w * chd : (w + 1) * chd]
            first = (s * 3 + q) * chd
            ts[first : first + chd, sign * CHUNK : (sign + 1) * CHUNK] = total.astype(bf16)

    for s in range(steps):
        res = dot(xs[s], edge_ref[...])
        add_terms(1, s, res[:rows, :128] + res[rows:, 128:], res[rows:, :128] - res[:rows, 128:])
    oe[...] = dot(wmat[...], ts[:, CHUNK:])

    def compute(u, m):
        res = dot(xs[0], tab[u, m])
        for s in range(steps):
            later = dot(xs[s + 1], tab[u, m]) if s + 1 < steps else None
            a, c = res[:rows, :CHUNK], res[:rows, CHUNK:]
            d, b = res[rows:, :CHUNK], res[rows:, CHUNK:]
            add_terms(0, s, a - b, c + d)
            add_terms(1, s, a + b, d - c)
            res = later
        pos = blocks + m
        neg = blocks - 1 - m
        part = p1.shape[3:]
        value = dot(wmat[...], ts[...])
        p1[u, pos % 2, pos // 2] = value[:, :CHUNK].reshape(part).astype(bf16)
        lane = lax.broadcasted_iota(jnp.int32, (wmat.shape[0], CHUNK), 1)
        mirror = jnp.where((lane + u) == 0, oe[:, m : m + 1], value[:, CHUNK:])
        p1[u, neg % 2, neg // 2] = mirror.reshape(part).astype(bf16)

    def copy1(u):
        return remote(p1.at[u, 1 - w1], r1.at[u], s1.at[u], q1.at[u], dev1())

    def copy2(u, k):
        return remote(
            b2.at[u, lax.rem(w2 + k, g2)], r2.at[u, k - 1], s2.at[u, k - 1], q2.at[u, k - 1], dev2(k)
        )

    def copy3(u):
        return remote(b3.at[u, 1 - c1], r3.at[u], s3.at[u], q3.at[u], dev3())

    def copy4(u, k):
        return remote(
            b4.at[u, lax.rem(c2 + k, g4)], r4.at[u, k - 1], s4.at[u, k - 1], q4.at[u, k - 1], dev4(k)
        )

    def stage2(u):
        copy1(u).wait()
        for i in range(g2):
            b2[u, i] = (p1[u, w1, i].astype(f32) + r1[u, i].astype(f32)).astype(bf16)
        for k in range(1, g2):
            copy2(u, k).start()
        a2[u] = p1[u, w1, w2].astype(f32) + r1[u, w2].astype(f32)

    def stage3(u):
        for k in range(1, g2):
            copy2(u, k).wait()
        for i in range(2):
            total = a2[u, i]
            for k in range(1, g2):
                total = total + r2[u, k - 1, i].astype(f32)
            a3[u, i] = total
            b3[u, i] = total.astype(bf16)
        copy3(u).start()

    def stage4(u):
        copy3(u).wait()
        for i in range(g4):
            total = a3[u, c1, i] + r3[u, i].astype(f32)
            a4[u, i] = total
            b4[u, i] = total.astype(bf16)
        for k in range(1, g4):
            copy4(u, k).start()

    def stage5(u):
        for k in range(1, g4):
            copy4(u, k).wait()
        total = a4[u, c2]
        for k in range(1, g4):
            total = total + r4[u, k - 1].astype(f32)
        n = total.shape[0] // 3
        lin, pr, pi = total[:n], total[n : 2 * n], total[2 * n :]
        count = traces[:n, :]
        fin[u] = lin * lax.rsqrt(count) * ((pr * pr + pi * pi) / count)

    def turn(v, carry):
        @pl.when(v < units)
        def _():
            table_copy(v).wait()
            compute(v, 0)

        @pl.when((v >= 1) & (v < units + 1))
        def _():
            stage2(v - 1)

        @pl.when((v >= 2) & (v < units + 2))
        def _():
            stage3(v - 2)

        @pl.when((v >= 3) & (v < units + 3))
        def _():
            stage4(v - 3)

        @pl.when(v >= 4)
        def _():
            stage5(v - 4)

        @pl.when(v < units)
        def _():
            for m in range(1, blocks):
                compute(v, m)
            copy1(v).start()

        return carry

    lax.fori_loop(0, units + 4, turn, 0)

    ri = lax.broadcasted_iota(jnp.int32, (CHUNK, CHUNK), 0)
    rj = lax.broadcasted_iota(jnp.int32, (CHUNK, CHUNK), 1)
    flip = jnp.where(ri + rj == CHUNK, 1.0, 0.0).astype(bf16)
    lane = lax.broadcasted_iota(jnp.int32, fin.shape[1:], 1)
    for u in range(units):
        value = fin[units - 1 - u]
        hi = value.astype(bf16)
        rest = value - hi.astype(f32)
        mid = rest.astype(bf16)
        low = (rest - mid.astype(f32)).astype(bf16)
        value = dot(hi, flip) + dot(mid, flip) + dot(low, flip)
        value = jnp.where(lane == 0, fin[(units - u) % units], value)
        value = jnp.where(lane * 0 + me_w < blocks, value, fin[u])
        for s in range(steps):
            o_ref[s, :, u * CHUNK : (u + 1) * CHUNK] = value[s * bl : (s + 1) * bl]


def shards(spectra, sources, bin_rows):
    chd, wd = spectra.shape[0], spectra.shape[1]
    steps = sources.shape[0]
    nchan, nwin = lax.axis_size("chan"), lax.axis_size("win")
    lag_dev = LAGS // nwin
    units, blocks = lag_dev // CHUNK, nwin // 2
    bl = NBINS // nchan
    rows = wd * chd
    g2, g4 = nwin // 2, nchan // 2
    x = jnp.transpose(spectra, (2, 1, 0, 3)).reshape(2, rows, F)

    table, edge = lag_tables(lag_dev)
    per = NBINS * 3 * steps // nchan
    piece = 2 * F // nchan
    tail = (per, CHUNK)
    cfg = (nchan, nwin, steps, wd, chd, units, blocks)
    dma = pltpu.SemaphoreType.DMA
    vmem = pl.BlockSpec(memory_space=pltpu.VMEM)
    return pl.pallas_call(
        functools.partial(kernel, cfg),
        out_shape=jax.ShapeDtypeStruct((steps, bl, lag_dev), f32),
        in_specs=[vmem, pl.BlockSpec(memory_space=pltpu.SMEM), vmem, vmem] + [pl.BlockSpec(memory_space=pl.ANY)],
        out_specs=vmem,
        scratch_shapes=[
            pltpu.VMEM((units, blocks, F, 2 * CHUNK), bf16),
            pltpu.VMEM((nchan, steps * wd, piece + 128), bf16),
            pltpu.VMEM((nchan - 1, steps * wd, piece + 128), bf16),
            pltpu.VMEM((nchan, steps * wd, piece), bf16),
            pltpu.VMEM((rows, F), bf16),
            pltpu.VMEM((rows, F), bf16),
            pltpu.VMEM((steps * wd, F), f32),
            pltpu.VMEM((steps * wd, F), f32),
            pltpu.VMEM((steps, 2 * rows, F), bf16),
            pltpu.VMEM((NBINS * 3 * steps, 3 * steps * chd), bf16),
            pltpu.VMEM((3 * steps * chd, 2 * CHUNK), bf16),
            pltpu.VMEM((NBINS * 3 * steps, 128), f32),
            pltpu.VMEM((steps * wd, 128), f32),
            pltpu.VMEM((units, steps * bl, CHUNK), f32),
            pltpu.VMEM((units, 2, g2, 2, g4) + tail, bf16),
            pltpu.VMEM((units, g2, 2, g4) + tail, bf16),
            pltpu.VMEM((units, 2, g4) + tail, f32),
            pltpu.VMEM((units, g2, 2, g4) + tail, bf16),
            pltpu.VMEM((units, g2 - 1, 2, g4) + tail, bf16),
            pltpu.VMEM((units, 2, g4) + tail, f32),
            pltpu.VMEM((units, 2, g4) + tail, bf16),
            pltpu.VMEM((units, g4) + tail, bf16),
            pltpu.VMEM((units, g4) + tail, f32),
            pltpu.VMEM((units, g4) + tail, bf16),
            pltpu.VMEM((units, g4 - 1) + tail, bf16),
            dma((units,)),
            dma((nchan - 1,)), dma((nchan - 1,)), dma((nchan - 1,)), dma((nchan - 1,)),
            dma((units,)), dma((units,)),
            dma((units, g2 - 1)), dma((units, g2 - 1)),
            dma((units,)), dma((units,)),
            dma((units, g4 - 1)), dma((units, g4 - 1)),
        ],
        compiler_params=pltpu.CompilerParams(
            collective_id=0, has_side_effects=True, vmem_limit_bytes=56 * 1024 * 1024
        ),
        name="stack",
    )(x, sources, bin_rows[:, 0], jnp.asarray(edge), jnp.asarray(table))


def solution(mesh):
    in_specs = (P("chan", "win", None, None), P(), P(None, "chan", None, None))
    out_specs = P(None, "chan", "win")
    return jax.shard_map(shards, mesh=mesh, in_specs=in_specs, out_specs=out_specs, check_vma=False)
```

```python
import functools

import jax
import jax.numpy as jnp
import ml_dtypes
import numpy as np
from jax import lax
from jax.experimental import pallas as pl
from jax.experimental.pallas import tpu as pltpu
from jax.sharding import PartitionSpec as P

F = 1024
F0 = 32
NFFT = 8192
LMAX = 2048
HW = 32
NBINS = 32
MOST = 3
LAGS = 4096
CHUNK = 128

epsilon_amp = 1e-06
phase_floor = 0.1

f32 = jnp.float32
bf16 = jnp.bfloat16
MESH = pl.DeviceIdType.MESH


def lag_tables(lag_dev):
    blocks = LMAX // lag_dev
    units = lag_dev // CHUNK
    freq = F0 + np.arange(F, dtype=np.int64)

    def trig(lags):
        turn = (freq[:, None] * lags[None, :]) % NFFT
        angle = turn * (2.0 * np.pi / NFFT)
        scale = F ** -0.5
        return np.cos(angle).astype(ml_dtypes.bfloat16), np.sin(angle).astype(ml_dtypes.bfloat16), scale

    table = np.zeros((units, blocks, F, 2 * CHUNK), ml_dtypes.bfloat16)
    for u in range(units):
        for m in range(blocks):
            cosine, sine, scale = trig(m * lag_dev + u * CHUNK + np.arange(CHUNK))
            both = np.concatenate([cosine, sine], axis=1).astype(np.float32) * scale
            table[u, m] = both.astype(ml_dtypes.bfloat16)
    edge = np.zeros((F, 256), np.float32)
    cosine, sine, scale = trig((np.arange(blocks) + 1) * lag_dev)
    edge[:, :blocks] = cosine.astype(np.float32) * scale
    edge[:, 128 : 128 + blocks] = sine.astype(np.float32) * scale
    return table, edge.astype(ml_dtypes.bfloat16)


def dot(a, b):
    return jnp.dot(a, b, preferred_element_type=f32)


def smooth_band(amp, band):
    hi = amp.astype(bf16)
    lo = (amp - hi.astype(f32)).astype(bf16)
    count = F // 256
    parts = []
    for j in range(count):
        first, last = max(j - 1, 0), min(j + 2, count)
        piece = band[(first - j + 1) * 256 : (last - j + 1) * 256, :]
        cols = slice(first * 256, last * 256)
        parts.append(dot(hi[:, cols], piece) + dot(lo[:, cols], piece))
    return jnp.concatenate(parts, axis=1) * (1.0 / (2 * HW + 1)) + epsilon_amp


def whiten(re, im, band):
    inv = 1.0 / smooth_band(jnp.sqrt(re * re + im * im), band)
    return (re * inv).astype(bf16), (im * inv).astype(bf16)


def kernel(
    cfg,
    x_ref, sources_ref, bins_ref, edge_ref, tab_hbm,
    o_ref,
    tab, sbuf, rsr, ag, wr_s, wi_s, sr_s, si_s, xs, wmat, ts, oe, traces, fin, res_a, res_b,
    p1, r1, a2, b2, r2, a3, b3, r3, a4, b4, r4,
    tab_sem, rs_s, rs_r, ag_s, ag_r, s1, q1, s2, q2, s3, q3, s4, q4,
):
    nchan, nwin, steps, wd, chd, units, blocks = cfg
    g2, g4 = nwin // 2, nchan // 2
    rows = wd * chd
    me_c, me_w = lax.axis_index("chan"), lax.axis_index("win")
    w1, w2 = lax.rem(me_w, 2), me_w // 2
    c1, c2 = lax.rem(me_c, 2), me_c // 2

    def chan_dev(k):
        return (lax.rem(me_c + k, nchan), me_w)

    def dev1():
        return (me_c, me_w + 1 - 2 * w1)

    def dev2(k):
        return (me_c, lax.rem(w2 + k, g2) * 2 + w1)

    def dev3():
        return (me_c + 1 - 2 * c1, me_w)

    def dev4(k):
        return (lax.rem(c2 + k, g4) * 2 + c1, me_w)

    def table_copy(u):
        return pltpu.make_async_copy(tab_hbm.at[u], tab.at[u], tab_sem.at[u])

    def remote(src, dst, s, r, dev):
        return pltpu.make_async_remote_copy(
            src_ref=src, dst_ref=dst, send_sem=s, recv_sem=r, device_id=dev, device_id_type=MESH
        )

    for u in range(units):
        table_copy(u).start()

    barrier = pltpu.get_barrier_semaphore()
    partners = [chan_dev(k) for k in range(1, nchan)] + [dev1()] + [dev2(k) for k in range(1, g2)]
    for dev in partners:
        pl.semaphore_signal(barrier, inc=1, device_id=dev, device_id_type=MESH)

    piece = 2 * F // nchan
    bl = NBINS // nchan
    row = lax.broadcasted_iota(jnp.int32, (steps * wd, rows), 0)
    col = lax.broadcasted_iota(jnp.int32, (steps * wd, rows), 1)
    want = jnp.full(row.shape, -1, jnp.int32)
    for s in range(steps):
        loc = sources_ref[s] - me_c * chd
        loc = jnp.where((loc >= 0) & (loc < chd), loc, -wd * chd - 1)
        want = jnp.where(row // wd == s, (row % wd) * chd + loc, want)
    pick = jnp.where(col == want, 1.0, 0.0).astype(bf16)
    both = jnp.concatenate([dot(pick, x_ref[0]), dot(pick, x_ref[1])], axis=1).astype(bf16)
    slots = bins_ref[...].astype(f32)
    live = jnp.where(slots >= 0.0, 1.0, 0.0).astype(bf16)

    def bins_of(shape, dims):
        i = lax.broadcasted_iota(jnp.int32, shape, len(shape) - 2)
        b = sum(lax.broadcasted_iota(jnp.int32, shape, d) * size for d, size in dims) * bl + i % bl
        hit = lax.broadcasted_iota(jnp.int32, shape, len(shape) - 1) == b
        return jnp.where(hit, 1.0, 0.0).reshape(-1, NBINS).astype(bf16), (i // bl).reshape(-1, NBINS)[:, 0:1]

    def pick_slots(chosen, values):
        return lax.dot_general(chosen, values, (((1,), (1,)), ((), ())), preferred_element_type=f32)

    chosen, step = bins_of((nchan, steps * bl, NBINS), [(0, 1)])
    cnt = pick_slots(chosen, live)
    col = lax.broadcasted_iota(jnp.int32, cnt.shape, 1)
    cnt = jnp.sum(jnp.where(col // MOST == step, cnt, 0.0), axis=1, keepdims=True)
    cnt = jnp.broadcast_to(cnt, (nchan * steps * bl, 128)).astype(bf16)
    for d in range(nchan):
        sbuf[d, :, :piece] = both[:, d * piece : (d + 1) * piece]
        sbuf[d, :, piece:] = jnp.zeros((steps * wd, 128), bf16)
        sbuf[d, : steps * bl, piece:] = cnt[d * steps * bl : (d + 1) * steps * bl]
    pl.semaphore_wait(barrier, len(partners))

    def rs_copy(k):
        return remote(
            sbuf.at[lax.rem(me_c + k, nchan)], rsr.at[k - 1], rs_s.at[k - 1], rs_r.at[k - 1], chan_dev(k)
        )

    def ag_copy(k):
        return remote(ag.at[me_c], ag.at[me_c], ag_s.at[k - 1], ag_r.at[k - 1], chan_dev(k))

    for k in range(1, nchan):
        rs_copy(k).start()

    bi = lax.broadcasted_iota(jnp.int32, (768, 256), 0)
    bj = lax.broadcasted_iota(jnp.int32, (768, 256), 1)
    band = jnp.where(jnp.abs(bi - 256 - bj) <= HW, 1.0, 0.0).astype(bf16)
    wr, wi = whiten(x_ref[0].astype(f32), x_ref[1].astype(f32), band)
    wr_s[...] = wr
    wi_s[...] = wi

    for k in range(1, nchan):
        rs_copy(k).wait()
    total = sbuf[me_c].astype(f32)
    for k in range(1, nchan):
        total = total + rsr[k - 1].astype(f32)
    ag[me_c] = total[:, :piece].astype(bf16)
    traces[...] = jnp.maximum(total[:, piece:], 1.0) * (wd * nwin)
    for k in range(1, nchan):
        ag_copy(k).start()

    shape = (2, g4, 3, steps * bl, NBINS)
    chosen, step = bins_of(shape, [(0, 1), (1, 2)])
    term = lax.broadcasted_iota(jnp.int32, shape, 2).reshape(-1, NBINS)[:, 0:1]
    offset = ((step * 3 + term) * chd).astype(f32)
    slots_at = pick_slots(chosen, slots.astype(bf16))
    wcol = lax.broadcasted_iota(jnp.int32, wmat.shape, 1).astype(f32)
    hit = wcol < 0.0
    for k in range(MOST):
        row_at = slots_at[:, k : k + 1]
        for s in range(1, steps):
            row_at = jnp.where(step == s, slots_at[:, s * MOST + k : s * MOST + k + 1], row_at)
        hit = hit | (wcol == jnp.where(row_at >= 0.0, row_at + offset, -1.0))
    wmat[...] = jnp.where(hit, 1.0, 0.0).astype(bf16)

    for k in range(1, nchan):
        ag_copy(k).wait()
    half = nchan // 2
    sre = jnp.concatenate([ag[d] for d in range(half)], axis=1).astype(f32)
    sim = jnp.concatenate([ag[d] for d in range(half, nchan)], axis=1).astype(f32)
    sr, si = whiten(sre, sim, band)
    sr_s[...] = sr.astype(f32)
    si_s[...] = si.astype(f32)

    for w in range(wd):
        here = slice(w * chd, (w + 1) * chd)
        wrw = wr_s[here, :].astype(f32)
        wiw = wi_s[here, :].astype(f32)
        for s in range(steps):
            i = s * wd + w
            a, b = sr_s[i : i + 1, :], si_s[i : i + 1, :]
            first = 2 * s * rows + w * chd
            xs[first : first + chd, :] = (wrw * a + wiw * b).astype(bf16)
            xs[first + rows : first + rows + chd, :] = (wiw * a - wrw * b).astype(bf16)

    tile = 16

    def add_terms(res, signs):
        for s in range(steps):
            for r in range(0, chd, tile):
                sums = [None] * 6
                for w in range(wd):
                    top = 2 * s * rows + w * chd + r
                    a, c = res[top : top + tile, :CHUNK], res[top : top + tile, CHUNK:]
                    top += rows
                    d, b = res[top : top + tile, :CHUNK], res[top : top + tile, CHUNK:]
                    for sign in signs:
                        re, im = (a + b, d - c) if sign else (a - b, c + d)
                        inv = lax.rsqrt(jnp.maximum(re * re + im * im, phase_floor * phase_floor))
                        for q, value in enumerate((re, re * inv, im * inv)):
                            n = sign * 3 + q
                            sums[n] = value if w == 0 else sums[n] + value
                for sign in signs:
                    for q in range(3):
                        first = (s * 3 + q) * chd + r
                        at = slice(sign * CHUNK, (sign + 1) * CHUNK)
                        ts[first : first + tile, at] = sums[sign * 3 + q].astype(bf16)

    res_a[...] = dot(xs[...], edge_ref[...])
    add_terms(res_a, (1,))
    oe[...] = dot(wmat[...], ts[:, CHUNK:])

    both_res = (res_a, res_b)

    def correlate(u, m):
        both_res[m % 2][...] = dot(xs[...], tab[u, m])

    def bin_sums(u, m):
        add_terms(both_res[m % 2], (0, 1))
        pos = blocks + m
        neg = blocks - 1 - m
        part = p1.shape[3:]
        value = dot(wmat[...], ts[...])
        p1[u, pos % 2, pos // 2] = value[:, :CHUNK].reshape(part).astype(bf16)
        lane = lax.broadcasted_iota(jnp.int32, (wmat.shape[0], CHUNK), 1)
        mirror = jnp.where((lane + u) == 0, oe[:, m : m + 1], value[:, CHUNK:])
        p1[u, neg % 2, neg // 2] = mirror.reshape(part).astype(bf16)

    def copy1(u):
        return remote(p1.at[u, 1 - w1], r1.at[u], s1.at[u], q1.at[u], dev1())

    def copy2(u, k):
        return remote(
            b2.at[u, lax.rem(w2 + k, g2)], r2.at[u, k - 1], s2.at[u, k - 1], q2.at[u, k - 1], dev2(k)
        )

    def copy3(u):
        return remote(b3.at[u, 1 - c1], r3.at[u], s3.at[u], q3.at[u], dev3())

    def copy4(u, k):
        return remote(
            b4.at[u, lax.rem(c2 + k, g4)], r4.at[u, k - 1], s4.at[u, k - 1], q4.at[u, k - 1], dev4(k)
        )

    def stage2(u):
        copy1(u).wait()
        for i in range(g2):
            b2[u, i] = (p1[u, w1, i].astype(f32) + r1[u, i].astype(f32)).astype(bf16)
        for k in range(1, g2):
            copy2(u, k).start()
        a2[u] = p1[u, w1, w2].astype(f32) + r1[u, w2].astype(f32)

    def stage3(u):
        for k in range(1, g2):
            copy2(u, k).wait()
        for i in range(2):
            total = a2[u, i]
            for k in range(1, g2):
                total = total + r2[u, k - 1, i].astype(f32)
            a3[u, i] = total
            b3[u, i] = total.astype(bf16)
        copy3(u).start()

    def stage4(u):
        copy3(u).wait()
        for i in range(g4):
            total = a3[u, c1, i] + r3[u, i].astype(f32)
            a4[u, i] = total
            b4[u, i] = total.astype(bf16)
        for k in range(1, g4):
            copy4(u, k).start()

    def stage5(u):
        for k in range(1, g4):
            copy4(u, k).wait()
        total = a4[u, c2]
        for k in range(1, g4):
            total = total + r4[u, k - 1].astype(f32)
        n = total.shape[0] // 3
        lin, pr, pi = total[:n], total[n : 2 * n], total[2 * n :]
        count = traces[:n, :]
        fin[u] = lin * lax.rsqrt(count) * ((pr * pr + pi * pi) / count)

    table_copy(0).wait()
    for m in range(blocks):
        correlate(0, m)
        if m:
            bin_sums(0, m - 1)

    def turn(v, carry):
        @pl.when(v < units)
        def _():
            table_copy(v).wait()
            for m in range(blocks):
                correlate(v, m)
                if m:
                    bin_sums(v, m - 1)
                else:
                    bin_sums(v - 1, blocks - 1)
                    copy1(v - 1).start()

        @pl.when(v == units)
        def _():
            bin_sums(v - 1, blocks - 1)
            copy1(v - 1).start()

        @pl.when(v < units + 1)
        def _():
            stage2(v - 1)

        @pl.when((v >= 2) & (v < units + 2))
        def _():
            stage3(v - 2)

        @pl.when((v >= 3) & (v < units + 3))
        def _():
            stage4(v - 3)

        @pl.when(v >= 4)
        def _():
            stage5(v - 4)

        return carry

    lax.fori_loop(1, units + 4, turn, 0)

    ri = lax.broadcasted_iota(jnp.int32, (CHUNK, CHUNK), 0)
    rj = lax.broadcasted_iota(jnp.int32, (CHUNK, CHUNK), 1)
    flip = jnp.where(ri + rj == CHUNK, 1.0, 0.0).astype(bf16)
    lane = lax.broadcasted_iota(jnp.int32, fin.shape[1:], 1)
    for u in range(units):
        value = fin[units - 1 - u]
        hi = value.astype(bf16)
        rest = value - hi.astype(f32)
        mid = rest.astype(bf16)
        low = (rest - mid.astype(f32)).astype(bf16)
        value = dot(hi, flip) + dot(mid, flip) + dot(low, flip)
        value = jnp.where(lane == 0, fin[(units - u) % units], value)
        value = jnp.where(lane * 0 + me_w < blocks, value, fin[u])
        o_ref[:, u * CHUNK : (u + 1) * CHUNK] = value


def shards(spectra, sources, bin_rows):
    chd, wd = spectra.shape[0], spectra.shape[1]
    steps = sources.shape[0]
    nchan, nwin = lax.axis_size("chan"), lax.axis_size("win")
    lag_dev = LAGS // nwin
    units, blocks = lag_dev // CHUNK, nwin // 2
    bl = NBINS // nchan
    rows = wd * chd
    g2, g4 = nwin // 2, nchan // 2
    x = jnp.transpose(spectra, (2, 1, 0, 3)).reshape(2, rows, F)

    table, edge = lag_tables(lag_dev)
    per = NBINS * 3 * steps // nchan
    piece = 2 * F // nchan
    tail = (per, CHUNK)
    cfg = (nchan, nwin, steps, wd, chd, units, blocks)
    dma = pltpu.SemaphoreType.DMA
    vmem = pl.BlockSpec(memory_space=pltpu.VMEM)
    slots = jnp.transpose(bin_rows, (0, 3, 1, 2)).reshape(steps * MOST, NBINS)
    out = pl.pallas_call(
        functools.partial(kernel, cfg),
        out_shape=jax.ShapeDtypeStruct((steps * bl, lag_dev), f32),
        in_specs=[vmem, pl.BlockSpec(memory_space=pltpu.SMEM), vmem, vmem] + [pl.BlockSpec(memory_space=pl.ANY)],
        out_specs=vmem,
        scratch_shapes=[
            pltpu.VMEM((units, blocks, F, 2 * CHUNK), bf16),
            pltpu.VMEM((nchan, steps * wd, piece + 128), bf16),
            pltpu.VMEM((nchan - 1, steps * wd, piece + 128), bf16),
            pltpu.VMEM((nchan, steps * wd, piece), bf16),
            pltpu.VMEM((rows, F), bf16),
            pltpu.VMEM((rows, F), bf16),
            pltpu.VMEM((steps * wd, F), f32),
            pltpu.VMEM((steps * wd, F), f32),
            pltpu.VMEM((steps * 2 * rows, F), bf16),
            pltpu.VMEM((NBINS * 3 * steps, 3 * steps * chd), bf16),
            pltpu.VMEM((3 * steps * chd, 2 * CHUNK), bf16),
            pltpu.VMEM((NBINS * 3 * steps, 128), f32),
            pltpu.VMEM((steps * wd, 128), f32),
            pltpu.VMEM((units, steps * bl, CHUNK), f32),
            pltpu.VMEM((steps * 2 * rows, 2 * CHUNK), f32),
            pltpu.VMEM((steps * 2 * rows, 2 * CHUNK), f32),
            pltpu.VMEM((units, 2, g2, 2, g4) + tail, bf16),
            pltpu.VMEM((units, g2, 2, g4) + tail, bf16),
            pltpu.VMEM((units, 2, g4) + tail, f32),
            pltpu.VMEM((units, g2, 2, g4) + tail, bf16),
            pltpu.VMEM((units, g2 - 1, 2, g4) + tail, bf16),
            pltpu.VMEM((units, 2, g4) + tail, f32),
            pltpu.VMEM((units, 2, g4) + tail, bf16),
            pltpu.VMEM((units, g4) + tail, bf16),
            pltpu.VMEM((units, g4) + tail, f32),
            pltpu.VMEM((units, g4) + tail, bf16),
            pltpu.VMEM((units, g4 - 1) + tail, bf16),
            dma((units,)),
            dma((nchan - 1,)), dma((nchan - 1,)), dma((nchan - 1,)), dma((nchan - 1,)),
            dma((units,)), dma((units,)),
            dma((units, g2 - 1)), dma((units, g2 - 1)),
            dma((units,)), dma((units,)),
            dma((units, g4 - 1)), dma((units, g4 - 1)),
        ],
        compiler_params=pltpu.CompilerParams(
            collective_id=0, has_side_effects=True, vmem_limit_bytes=56 * 1024 * 1024
        ),
        name="stack",
    )(x, sources, slots, jnp.asarray(edge), jnp.asarray(table))
    return out.reshape(steps, bl, lag_dev)


def solution(mesh):
    in_specs = (P("chan", "win", None, None), P(), P(None, "chan", None, None))
    out_specs = P(None, "chan", "win")
    return jax.shard_map(shards, mesh=mesh, in_specs=in_specs, out_specs=out_specs, check_vma=False)
```

```python
import functools

import jax
import jax.numpy as jnp
import ml_dtypes
import numpy as np
from jax import lax
from jax.experimental import pallas as pl
from jax.experimental.pallas import tpu as pltpu
from jax.sharding import PartitionSpec as P

F = 1024
F0 = 32
NFFT = 8192
LMAX = 2048
HW = 32
NBINS = 32
MOST = 3
LAGS = 4096
CHUNK = 128

epsilon_amp = 1e-06
phase_floor = 0.1

f32 = jnp.float32
bf16 = jnp.bfloat16
MESH = pl.DeviceIdType.MESH


def lag_tables(lag_dev):
    blocks = LMAX // 2 // lag_dev
    units = lag_dev // CHUNK
    freq = F0 + np.arange(F, dtype=np.int64)

    def trig(lags):
        turn = (freq[:, None] * lags[None, :]) % NFFT
        angle = turn * (2.0 * np.pi / NFFT)
        both = np.zeros((F, 256), np.float32)
        both[:, : lags.size] = np.cos(angle).astype(ml_dtypes.bfloat16)
        both[:, CHUNK : CHUNK + lags.size] = np.sin(angle).astype(ml_dtypes.bfloat16)
        both = (both * F ** -0.5).astype(ml_dtypes.bfloat16)
        return np.stack([both[m::4] for m in range(4)])

    starts = [[m * lag_dev + u * CHUNK for m in range(blocks)] for u in range(units)]
    table = np.stack([np.stack([trig(t + np.arange(CHUNK)) for t in at]) for at in starts])
    return table, trig((np.arange(blocks) + 1) * lag_dev)


def dot(a, b):
    return jnp.dot(a, b, preferred_element_type=f32)


def smooth_band(amp, band):
    hi = amp.astype(bf16)
    lo = (amp - hi.astype(f32)).astype(bf16)
    count = F // 256
    parts = []
    for j in range(count):
        first, last = max(j - 1, 0), min(j + 2, count)
        piece = band[(first - j + 1) * 256 : (last - j + 1) * 256, :]
        cols = slice(first * 256, last * 256)
        parts.append(dot(hi[:, cols], piece) + dot(lo[:, cols], piece))
    return jnp.concatenate(parts, axis=1) * (1.0 / (2 * HW + 1)) + epsilon_amp


def whiten(re, im, band):
    inv = 1.0 / smooth_band(jnp.sqrt(re * re + im * im), band)
    return (re * inv).astype(bf16), (im * inv).astype(bf16)


def kernel(
    cfg,
    x_ref, sources_ref, bins_ref, edge_ref, tab_hbm,
    o_ref,
    tab, sbuf, rsr, ag, wr_s, wi_s, sr_s, si_s, xs, wmat, ts, oe, traces, fin, res_a, res_b,
    p1, r1, a2, b2, r2, a3, b3, r3, a4, b4, r4,
    tab_sem, rs_s, rs_r, ag_s, ag_r, s1, q1, s2, q2, s3, q3, s4, q4,
):
    nchan, nwin, steps, wd, chd, units, blocks = cfg
    g2, g4 = nwin // 2, nchan // 2
    rows = wd * chd
    me_c, me_w = lax.axis_index("chan"), lax.axis_index("win")
    w1, w2 = lax.rem(me_w, 2), me_w // 2
    c1, c2 = lax.rem(me_c, 2), me_c // 2

    def chan_dev(k):
        return (lax.rem(me_c + k, nchan), me_w)

    def dev1():
        return (me_c, me_w + 1 - 2 * w1)

    def dev2(k):
        return (me_c, lax.rem(w2 + k, g2) * 2 + w1)

    def dev3():
        return (me_c + 1 - 2 * c1, me_w)

    def dev4(k):
        return (lax.rem(c2 + k, g4) * 2 + c1, me_w)

    def table_copy(u):
        return pltpu.make_async_copy(tab_hbm.at[u], tab.at[u], tab_sem.at[u])

    def remote(src, dst, s, r, dev):
        return pltpu.make_async_remote_copy(
            src_ref=src, dst_ref=dst, send_sem=s, recv_sem=r, device_id=dev, device_id_type=MESH
        )

    for u in range(units):
        table_copy(u).start()

    barrier = pltpu.get_barrier_semaphore()
    partners = [chan_dev(k) for k in range(1, nchan)] + [dev1()] + [dev2(k) for k in range(1, g2)]
    for dev in partners:
        pl.semaphore_signal(barrier, inc=1, device_id=dev, device_id_type=MESH)

    piece = 2 * F // nchan
    bl = NBINS // nchan
    row = lax.broadcasted_iota(jnp.int32, (steps * wd, rows), 0)
    col = lax.broadcasted_iota(jnp.int32, (steps * wd, rows), 1)
    want = jnp.full(row.shape, -1, jnp.int32)
    for s in range(steps):
        loc = sources_ref[s] - me_c * chd
        loc = jnp.where((loc >= 0) & (loc < chd), loc, -wd * chd - 1)
        want = jnp.where(row // wd == s, (row % wd) * chd + loc, want)
    pick = jnp.where(col == want, 1.0, 0.0).astype(bf16)
    both = jnp.concatenate([dot(pick, x_ref[0]), dot(pick, x_ref[1])], axis=1).astype(bf16)
    slots = [bins_ref[s].astype(f32) for s in range(steps)]

    def bins_of(shape, dims):
        i = lax.broadcasted_iota(jnp.int32, shape, len(shape) - 2)
        b = sum(lax.broadcasted_iota(jnp.int32, shape, d) * size for d, size in dims) * bl + i % bl
        hit = lax.broadcasted_iota(jnp.int32, shape, len(shape) - 1) == b
        return jnp.where(hit, 1.0, 0.0).reshape(-1, NBINS).astype(bf16), (i // bl).reshape(-1, NBINS)[:, 0:1]

    def pick_slots(chosen, values):
        return lax.dot_general(chosen, values, (((1,), (1,)), ((), ())), preferred_element_type=f32)

    chosen, step = bins_of((nchan, steps * bl, NBINS), [(0, 1)])
    cnt = jnp.zeros(step.shape, f32)
    for s in range(steps):
        live = pick_slots(chosen, jnp.where(slots[s] >= 0.0, 1.0, 0.0).astype(bf16))
        cnt = jnp.where(step == s, jnp.sum(live, axis=1, keepdims=True), cnt)
    cnt = jnp.broadcast_to(cnt, (nchan * steps * bl, 128)).astype(bf16)
    for d in range(nchan):
        sbuf[d, :, :piece] = both[:, d * piece : (d + 1) * piece]
        sbuf[d, :, piece:] = jnp.zeros((steps * wd, 128), bf16)
        sbuf[d, : steps * bl, piece:] = cnt[d * steps * bl : (d + 1) * steps * bl]
    pl.semaphore_wait(barrier, len(partners))

    def rs_copy(k):
        return remote(
            sbuf.at[lax.rem(me_c + k, nchan)], rsr.at[k - 1], rs_s.at[k - 1], rs_r.at[k - 1], chan_dev(k)
        )

    def ag_copy(k):
        return remote(ag.at[me_c], ag.at[me_c], ag_s.at[k - 1], ag_r.at[k - 1], chan_dev(k))

    for k in range(1, nchan):
        rs_copy(k).start()

    bi = lax.broadcasted_iota(jnp.int32, (768, 256), 0)
    bj = lax.broadcasted_iota(jnp.int32, (768, 256), 1)
    band = jnp.where(jnp.abs(bi - 256 - bj) <= HW, 1.0, 0.0).astype(bf16)
    wr, wi = whiten(x_ref[0].astype(f32), x_ref[1].astype(f32), band)
    pi_ = lax.broadcasted_iota(jnp.int32, (F, F), 0)
    pj = lax.broadcasted_iota(jnp.int32, (F, F), 1)
    order = jnp.where(pi_ == (pj % 256) * 4 + pj // 256, 1.0, 0.0).astype(bf16)
    wr_s[...] = dot(wr, order).astype(bf16)
    wi_s[...] = dot(wi, order).astype(bf16)

    for k in range(1, nchan):
        rs_copy(k).wait()
    total = sbuf[me_c].astype(f32)
    for k in range(1, nchan):
        total = total + rsr[k - 1].astype(f32)
    ag[me_c] = total[:, :piece].astype(bf16)
    traces[...] = jnp.maximum(total[:, piece:], 1.0) * (wd * nwin)
    for k in range(1, nchan):
        ag_copy(k).start()

    shape = (2, g4, 3, steps * bl, NBINS)
    chosen, step = bins_of(shape, [(0, 1), (1, 2)])
    term = lax.broadcasted_iota(jnp.int32, shape, 2).reshape(-1, NBINS)[:, 0:1]
    offset = ((step * 3 + term) * chd).astype(f32)
    slots_at = pick_slots(chosen, slots[0].astype(bf16))
    for s in range(1, steps):
        slots_at = jnp.where(step == s, pick_slots(chosen, slots[s].astype(bf16)), slots_at)
    slots_at = jnp.where(slots_at >= 0.0, slots_at + offset, -1.0)
    wcol = lax.broadcasted_iota(jnp.int32, wmat.shape, 1).astype(f32)
    hit = wcol < 0.0
    for k in range(MOST):
        hit = hit | (wcol == slots_at[:, k : k + 1])
    wmat[...] = jnp.where(hit, 1.0, 0.0).astype(bf16)

    for k in range(1, nchan):
        ag_copy(k).wait()
    half = nchan // 2
    sre = jnp.concatenate([ag[d] for d in range(half)], axis=1).astype(f32)
    sim = jnp.concatenate([ag[d] for d in range(half, nchan)], axis=1).astype(f32)
    sr, si = whiten(sre, sim, band)
    sr_s[...] = dot(sr, order)
    si_s[...] = dot(si, order)

    for w in range(wd):
        here = slice(w * chd, (w + 1) * chd)
        wrw = wr_s[here, :].astype(f32)
        wiw = wi_s[here, :].astype(f32)
        for s in range(steps):
            i = s * wd + w
            a, b = sr_s[i : i + 1, :], si_s[i : i + 1, :]
            first = 2 * s * rows + w * chd
            xs[first : first + chd, :] = (wrw * a + wiw * b).astype(bf16)
            xs[first + rows : first + rows + chd, :] = (wiw * a - wrw * b).astype(bf16)

    tile = 8
    lanes = (slice(0, CHUNK), slice(CHUNK, 2 * CHUNK))

    def lag_values(res, top, outs):
        g, h = [], []
        for m in range(4):
            a, c = res[m, top : top + tile, lanes[0]], res[m, top : top + tile, lanes[1]]
            d, b = res[m, top + rows : top + rows + tile, lanes[0]], res[m, top + rows : top + rows + tile, lanes[1]]
            g.append((a - b, c + d))
            h.append((a + b, d - c))
        values = {}
        for parts, plain, turned, sign in ((g, 0, 1, 1), (h, 2, 3, -1)):
            (r0, i0), (r1, i1), (r2, i2), (r3, i3) = parts
            if plain in outs:
                values[plain] = (r0 + r2) + (r1 + r3), (i0 + i2) + (i1 + i3)
            if turned in outs:
                ro, io = r1 - r3, i1 - i3
                if sign > 0:
                    values[turned] = (r0 - r2) + io, (i0 - i2) - ro
                else:
                    values[turned] = (r0 - r2) - io, (i0 - i2) + ro
        return values

    def add_terms(res, h, outs):
        for k in range(steps // 2):
            for r in range(0, chd, 2 * tile):
                halves = []
                for r8 in (r, r + tile):
                    sums = {}
                    for w in range(wd):
                        values = lag_values(res, 2 * k * rows + w * chd + r8, outs)
                        for out in outs:
                            re, im = values[out]
                            inv = lax.rsqrt(jnp.maximum(re * re + im * im, phase_floor * phase_floor))
                            for q, value in enumerate((re, re * inv, im * inv)):
                                sums[out, q] = value if w == 0 else sums[out, q] + value
                    halves.append(sums)
                for out in outs:
                    for q in range(3):
                        first = ((h * (steps // 2) + k) * 3 + q) * chd + r
                        value = jnp.concatenate([half[out, q] for half in halves], axis=0)
                        ts[first : first + 2 * tile, out * CHUNK : (out + 1) * CHUNK] = value.astype(bf16)

    both_res = (res_a, res_b)
    part_rows = steps * rows

    def correlate(table, h):
        for m in range(4):
            both_res[h][m] = dot(xs[h * part_rows : (h + 1) * part_rows, m * 256 : (m + 1) * 256], table[m])

    for h in range(2):
        correlate(edge_ref, h)
        add_terms(both_res[h], h, (2, 3))
    oe[...] = dot(wmat[...], ts[:, 2 * CHUNK :])

    def bin_sums(u, m, h):
        add_terms(both_res[h], h, (0, 1, 2, 3))
        if h == 0:
            return
        part = p1.shape[3:]
        value = dot(wmat[...], ts[...])
        lane = lax.broadcasted_iota(jnp.int32, (wmat.shape[0], CHUNK), 1)
        for out, w in enumerate((nwin // 2 + m, m, nwin // 2 - 1 - m, nwin - 1 - m)):
            piece_out = value[:, out * CHUNK : (out + 1) * CHUNK]
            if out >= 2:
                at = (out - 2) * CHUNK + m
                piece_out = jnp.where((lane + u) == 0, oe[:, at : at + 1], piece_out)
            p1[u, w % 2, w // 2] = piece_out.reshape(part).astype(bf16)

    def copy1(u):
        return remote(p1.at[u, 1 - w1], r1.at[u], s1.at[u], q1.at[u], dev1())

    def copy2(u, k):
        return remote(
            b2.at[u, lax.rem(w2 + k, g2)], r2.at[u, k - 1], s2.at[u, k - 1], q2.at[u, k - 1], dev2(k)
        )

    def copy3(u):
        return remote(b3.at[u, 1 - c1], r3.at[u], s3.at[u], q3.at[u], dev3())

    def copy4(u, k):
        return remote(
            b4.at[u, lax.rem(c2 + k, g4)], r4.at[u, k - 1], s4.at[u, k - 1], q4.at[u, k - 1], dev4(k)
        )

    def stage2(u):
        copy1(u).wait()
        for i in range(g2):
            b2[u, i] = (p1[u, w1, i].astype(f32) + r1[u, i].astype(f32)).astype(bf16)
        for k in range(1, g2):
            copy2(u, k).start()
        a2[u] = p1[u, w1, w2].astype(f32) + r1[u, w2].astype(f32)

    def stage3(u):
        for k in range(1, g2):
            copy2(u, k).wait()
        for i in range(2):
            total = a2[u, i]
            for k in range(1, g2):
                total = total + r2[u, k - 1, i].astype(f32)
            a3[u, i] = total
            b3[u, i] = total.astype(bf16)
        copy3(u).start()

    def stage4(u):
        copy3(u).wait()
        for i in range(g4):
            total = a3[u, c1, i] + r3[u, i].astype(f32)
            a4[u, i] = total
            b4[u, i] = total.astype(bf16)
        for k in range(1, g4):
            copy4(u, k).start()

    def stage5(u):
        for k in range(1, g4):
            copy4(u, k).wait()
        total = a4[u, c2]
        for k in range(1, g4):
            total = total + r4[u, k - 1].astype(f32)
        n = total.shape[0] // 3
        lin, pr, pi = total[:n], total[n : 2 * n], total[2 * n :]
        count = traces[:n, :]
        fin[u] = lin * lax.rsqrt(count) * ((pr * pr + pi * pi) / count)

    jobs = [(m, h) for m in range(blocks) for h in range(2)]
    table_copy(0).wait()
    for n, (m, h) in enumerate(jobs):
        correlate(tab.at[0, m], h)
        if n:
            bin_sums(0, *jobs[n - 1])

    def turn(v, carry):
        @pl.when(v < units)
        def _():
            table_copy(v).wait()
            for n, (m, h) in enumerate(jobs):
                correlate(tab.at[v, m], h)
                if n:
                    bin_sums(v, *jobs[n - 1])
                else:
                    bin_sums(v - 1, *jobs[-1])
                    copy1(v - 1).start()

        @pl.when(v == units)
        def _():
            bin_sums(v - 1, *jobs[-1])
            copy1(v - 1).start()

        @pl.when(v < units + 1)
        def _():
            stage2(v - 1)

        @pl.when((v >= 2) & (v < units + 2))
        def _():
            stage3(v - 2)

        @pl.when((v >= 3) & (v < units + 3))
        def _():
            stage4(v - 3)

        @pl.when(v >= 4)
        def _():
            stage5(v - 4)

        return carry

    lax.fori_loop(1, units + 4, turn, 0)

    ri = lax.broadcasted_iota(jnp.int32, (CHUNK, CHUNK), 0)
    rj = lax.broadcasted_iota(jnp.int32, (CHUNK, CHUNK), 1)
    flip = jnp.where(ri + rj == CHUNK, 1.0, 0.0).astype(bf16)
    lane = lax.broadcasted_iota(jnp.int32, fin.shape[1:], 1)
    for u in range(units):
        value = fin[units - 1 - u]
        hi = value.astype(bf16)
        rest = value - hi.astype(f32)
        mid = rest.astype(bf16)
        low = (rest - mid.astype(f32)).astype(bf16)
        value = dot(hi, flip) + dot(mid, flip) + dot(low, flip)
        value = jnp.where(lane == 0, fin[(units - u) % units], value)
        value = jnp.where((lane * 0 + me_w // blocks) % 2 == 1, value, fin[u])
        o_ref[:, u * CHUNK : (u + 1) * CHUNK] = value


def shards(spectra, sources, bin_rows):
    chd, wd = spectra.shape[0], spectra.shape[1]
    steps = sources.shape[0]
    nchan, nwin = lax.axis_size("chan"), lax.axis_size("win")
    lag_dev = LAGS // nwin
    units, blocks = lag_dev // CHUNK, nwin // 4
    bl = NBINS // nchan
    rows = wd * chd
    g2, g4 = nwin // 2, nchan // 2
    x = jnp.transpose(spectra, (2, 1, 0, 3)).reshape(2, rows, F)

    table, edge = lag_tables(lag_dev)
    per = NBINS * 3 * steps // nchan
    piece = 2 * F // nchan
    tail = (per, CHUNK)
    cfg = (nchan, nwin, steps, wd, chd, units, blocks)
    dma = pltpu.SemaphoreType.DMA
    vmem = pl.BlockSpec(memory_space=pltpu.VMEM)
    slots = jnp.transpose(bin_rows[:, 0], (0, 2, 1))
    out = pl.pallas_call(
        functools.partial(kernel, cfg),
        out_shape=jax.ShapeDtypeStruct((steps * bl, lag_dev), f32),
        in_specs=[vmem, pl.BlockSpec(memory_space=pltpu.SMEM), vmem, vmem] + [pl.BlockSpec(memory_space=pl.ANY)],
        out_specs=vmem,
        scratch_shapes=[
            pltpu.VMEM((units, blocks, 4, F // 4, 2 * CHUNK), bf16),
            pltpu.VMEM((nchan, steps * wd, piece + 128), bf16),
            pltpu.VMEM((nchan - 1, steps * wd, piece + 128), bf16),
            pltpu.VMEM((nchan, steps * wd, piece), bf16),
            pltpu.VMEM((rows, F), bf16),
            pltpu.VMEM((rows, F), bf16),
            pltpu.VMEM((steps * wd, F), f32),
            pltpu.VMEM((steps * wd, F), f32),
            pltpu.VMEM((steps * 2 * rows, F), bf16),
            pltpu.VMEM((NBINS * 3 * steps, 3 * steps * chd), bf16),
            pltpu.VMEM((3 * steps * chd, 4 * CHUNK), bf16),
            pltpu.VMEM((NBINS * 3 * steps, 2 * CHUNK), f32),
            pltpu.VMEM((steps * wd, 128), f32),
            pltpu.VMEM((units, steps * bl, CHUNK), f32),
            pltpu.VMEM((4, steps * rows, 2 * CHUNK), f32),
            pltpu.VMEM((4, steps * rows, 2 * CHUNK), f32),
            pltpu.VMEM((units, 2, g2, 2, g4) + tail, bf16),
            pltpu.VMEM((units, g2, 2, g4) + tail, bf16),
            pltpu.VMEM((units, 2, g4) + tail, f32),
            pltpu.VMEM((units, g2, 2, g4) + tail, bf16),
            pltpu.VMEM((units, g2 - 1, 2, g4) + tail, bf16),
            pltpu.VMEM((units, 2, g4) + tail, f32),
            pltpu.VMEM((units, 2, g4) + tail, bf16),
            pltpu.VMEM((units, g4) + tail, bf16),
            pltpu.VMEM((units, g4) + tail, f32),
            pltpu.VMEM((units, g4) + tail, bf16),
            pltpu.VMEM((units, g4 - 1) + tail, bf16),
            dma((units,)),
            dma((nchan - 1,)), dma((nchan - 1,)), dma((nchan - 1,)), dma((nchan - 1,)),
            dma((units,)), dma((units,)),
            dma((units, g2 - 1)), dma((units, g2 - 1)),
            dma((units,)), dma((units,)),
            dma((units, g4 - 1)), dma((units, g4 - 1)),
        ],
        compiler_params=pltpu.CompilerParams(
            collective_id=0, has_side_effects=True, vmem_limit_bytes=56 * 1024 * 1024
        ),
        name="stack",
    )(x, sources, slots, jnp.asarray(edge), jnp.asarray(table))
    return out.reshape(steps, bl, lag_dev)


def solution(mesh):
    in_specs = (P("chan", "win", None, None), P(), P(None, "chan", None, None))
    out_specs = P(None, "chan", "win")
    return jax.shard_map(shards, mesh=mesh, in_specs=in_specs, out_specs=out_specs, check_vma=False)
```

```python
import functools

import jax
import jax.numpy as jnp
import ml_dtypes
import numpy as np
from jax import lax
from jax.experimental import pallas as pl
from jax.experimental.pallas import tpu as pltpu
from jax.sharding import PartitionSpec as P

F = 1024
F0 = 32
NFFT = 8192
LMAX = 2048
HW = 32
NBINS = 32
MOST = 3
LAGS = 4096
CHUNK = 128

epsilon_amp = 1e-06
phase_floor = 0.1

f32 = jnp.float32
bf16 = jnp.bfloat16
MESH = pl.DeviceIdType.MESH


def lag_tables(lag_dev):
    blocks = LMAX // 2 // lag_dev
    units = lag_dev // CHUNK
    freq = F0 + np.arange(F, dtype=np.int64)

    def trig(lags):
        turn = (freq[:, None] * lags[None, :]) % NFFT
        angle = turn * (2.0 * np.pi / NFFT)
        both = np.zeros((F, 256), np.float32)
        both[:, : lags.size] = np.cos(angle).astype(ml_dtypes.bfloat16)
        both[:, CHUNK : CHUNK + lags.size] = np.sin(angle).astype(ml_dtypes.bfloat16)
        both = (both * F ** -0.5).astype(ml_dtypes.bfloat16)
        return np.stack([both[m::4] for m in range(4)])

    starts = [[m * lag_dev + u * CHUNK for m in range(blocks)] for u in range(units)]
    table = np.stack([np.stack([trig(t + np.arange(CHUNK)) for t in at]) for at in starts])
    return table, trig((np.arange(blocks) + 1) * lag_dev)


def dot(a, b):
    return jnp.dot(a, b, preferred_element_type=f32)


def smooth_band(amp, band):
    hi = amp.astype(bf16)
    lo = (amp - hi.astype(f32)).astype(bf16)
    count = F // 256
    parts = []
    for j in range(count):
        first, last = max(j - 1, 0), min(j + 2, count)
        piece = band[(first - j + 1) * 256 : (last - j + 1) * 256, :]
        cols = slice(first * 256, last * 256)
        parts.append(dot(hi[:, cols], piece) + dot(lo[:, cols], piece))
    return jnp.concatenate(parts, axis=1) * (1.0 / (2 * HW + 1)) + epsilon_amp


def whiten(re, im, band):
    inv = 1.0 / smooth_band(jnp.sqrt(re * re + im * im), band)
    return (re * inv).astype(bf16), (im * inv).astype(bf16)


def kernel(
    cfg,
    x_ref, sources_ref, bins_ref, edge_ref, tab_hbm,
    o_ref,
    tab, sbuf, rsr, ag, wr_s, wi_s, sr_s, si_s, xs, wmat, ts, oe, traces, fin, res_a, res_b,
    p1, r1, a2, b2, r2, a3, b3, r3, a4, b4, r4, a3o, b3o, r3o, b2o, r2o,
    tab_sem, rs_s, rs_r, ag_s, ag_r, s1, q1, s2, q2, s3, q3, s4, q4,
):
    nchan, nwin, steps, wd, chd, units, blocks = cfg
    g2, g4 = nwin // 2, nchan // 2
    rows = wd * chd
    me_c, me_w = lax.axis_index("chan"), lax.axis_index("win")
    w1, w2 = lax.rem(me_w, 2), me_w // 2
    c1, c2 = lax.rem(me_c, 2), me_c // 2

    def chan_dev(k):
        return (lax.rem(me_c + k, nchan), me_w)

    def dev1():
        return (me_c, me_w + 1 - 2 * w1)

    def dev2(k):
        return (me_c, lax.rem(w2 + k, g2) * 2 + w1)

    def dev3():
        return (me_c + 1 - 2 * c1, me_w)

    def dev4(k):
        return (lax.rem(c2 + k, g4) * 2 + c1, me_w)

    def table_copy(u):
        return pltpu.make_async_copy(tab_hbm.at[u], tab.at[u], tab_sem.at[u])

    def remote(src, dst, s, r, dev):
        return pltpu.make_async_remote_copy(
            src_ref=src, dst_ref=dst, send_sem=s, recv_sem=r, device_id=dev, device_id_type=MESH
        )

    for u in range(units):
        table_copy(u).start()

    barrier = pltpu.get_barrier_semaphore()
    partners = [chan_dev(k) for k in range(1, nchan)] + [dev1()] + [dev2(k) for k in range(1, g2)]
    for dev in partners:
        pl.semaphore_signal(barrier, inc=1, device_id=dev, device_id_type=MESH)

    piece = 2 * F // nchan
    bl = NBINS // nchan
    row = lax.broadcasted_iota(jnp.int32, (steps * wd, rows), 0)
    col = lax.broadcasted_iota(jnp.int32, (steps * wd, rows), 1)
    want = jnp.full(row.shape, -1, jnp.int32)
    for s in range(steps):
        loc = sources_ref[s] - me_c * chd
        loc = jnp.where((loc >= 0) & (loc < chd), loc, -wd * chd - 1)
        want = jnp.where(row // wd == s, (row % wd) * chd + loc, want)
    pick = jnp.where(col == want, 1.0, 0.0).astype(bf16)
    both = jnp.concatenate([dot(pick, x_ref[0]), dot(pick, x_ref[1])], axis=1).astype(bf16)
    slots = [bins_ref[s].astype(f32) for s in range(steps)]

    def bins_of(shape, dims):
        i = lax.broadcasted_iota(jnp.int32, shape, len(shape) - 2)
        b = sum(lax.broadcasted_iota(jnp.int32, shape, d) * size for d, size in dims) * bl + i % bl
        hit = lax.broadcasted_iota(jnp.int32, shape, len(shape) - 1) == b
        return jnp.where(hit, 1.0, 0.0).reshape(-1, NBINS).astype(bf16), (i // bl).reshape(-1, NBINS)[:, 0:1]

    def pick_slots(chosen, values):
        return lax.dot_general(chosen, values, (((1,), (1,)), ((), ())), preferred_element_type=f32)

    chosen, step = bins_of((nchan, steps * bl, NBINS), [(0, 1)])
    cnt = jnp.zeros(step.shape, f32)
    for s in range(steps):
        live = pick_slots(chosen, jnp.where(slots[s] >= 0.0, 1.0, 0.0).astype(bf16))
        cnt = jnp.where(step == s, jnp.sum(live, axis=1, keepdims=True), cnt)
    cnt = jnp.broadcast_to(cnt, (nchan * steps * bl, 128)).astype(bf16)
    for d in range(nchan):
        sbuf[d, :, :piece] = both[:, d * piece : (d + 1) * piece]
        sbuf[d, :, piece:] = jnp.zeros((steps * wd, 128), bf16)
        sbuf[d, : steps * bl, piece:] = cnt[d * steps * bl : (d + 1) * steps * bl]
    pl.semaphore_wait(barrier, len(partners))

    def rs_copy(k):
        return remote(
            sbuf.at[lax.rem(me_c + k, nchan)], rsr.at[k - 1], rs_s.at[k - 1], rs_r.at[k - 1], chan_dev(k)
        )

    def ag_copy(k):
        return remote(ag.at[me_c], ag.at[me_c], ag_s.at[k - 1], ag_r.at[k - 1], chan_dev(k))

    for k in range(1, nchan):
        rs_copy(k).start()

    bi = lax.broadcasted_iota(jnp.int32, (768, 256), 0)
    bj = lax.broadcasted_iota(jnp.int32, (768, 256), 1)
    band = jnp.where(jnp.abs(bi - 256 - bj) <= HW, 1.0, 0.0).astype(bf16)
    wr, wi = whiten(x_ref[0].astype(f32), x_ref[1].astype(f32), band)
    pi_ = lax.broadcasted_iota(jnp.int32, (F, F), 0)
    pj = lax.broadcasted_iota(jnp.int32, (F, F), 1)
    order = jnp.where(pi_ == (pj & 255) * 4 + (pj >> 8), 1.0, 0.0).astype(bf16)
    wr_s[...] = dot(wr, order).astype(bf16)
    wi_s[...] = dot(wi, order).astype(bf16)

    for k in range(1, nchan):
        rs_copy(k).wait()
    total = sbuf[me_c].astype(f32)
    for k in range(1, nchan):
        total = total + rsr[k - 1].astype(f32)
    ag[me_c] = total[:, :piece].astype(bf16)
    traces[...] = jnp.maximum(total[:, piece:], 1.0) * (wd * nwin)
    for k in range(1, nchan):
        ag_copy(k).start()

    shape = (2, g4, 3, steps * bl, NBINS)
    chosen, step = bins_of(shape, [(0, 1), (1, 2)])
    term = lax.broadcasted_iota(jnp.int32, shape, 2).reshape(-1, NBINS)[:, 0:1]
    offset = ((step * 3 + term) * chd).astype(f32)
    slots_at = pick_slots(chosen, slots[0].astype(bf16))
    for s in range(1, steps):
        slots_at = jnp.where(step == s, pick_slots(chosen, slots[s].astype(bf16)), slots_at)
    slots_at = jnp.where(slots_at >= 0.0, slots_at + offset, -1.0)
    wcol = lax.broadcasted_iota(jnp.int32, wmat.shape, 1).astype(f32)
    hit = wcol < 0.0
    for k in range(MOST):
        hit = hit | (wcol == slots_at[:, k : k + 1])
    wmat[...] = jnp.where(hit, 1.0, 0.0).astype(bf16)

    for k in range(1, nchan):
        ag_copy(k).wait()
    half = nchan // 2
    sre = jnp.concatenate([ag[d] for d in range(half)], axis=1).astype(f32)
    sim = jnp.concatenate([ag[d] for d in range(half, nchan)], axis=1).astype(f32)
    sr, si = whiten(sre, sim, band)
    sr_s[...] = dot(sr, order)
    si_s[...] = dot(si, order)

    for w in range(wd):
        here = slice(w * chd, (w + 1) * chd)
        wrw = wr_s[here, :].astype(f32)
        wiw = wi_s[here, :].astype(f32)
        for s in range(steps):
            i = s * wd + w
            a, b = sr_s[i : i + 1, :], si_s[i : i + 1, :]
            first = 2 * s * rows + w * chd
            xs[first : first + chd, :] = (wrw * a + wiw * b).astype(bf16)
            xs[first + rows : first + rows + chd, :] = (wiw * a - wrw * b).astype(bf16)

    tile = 8
    lanes = (slice(0, CHUNK), slice(CHUNK, 2 * CHUNK))

    def lag_values(res, top, outs):
        g, h = [], []
        for m in range(4):
            a, c = res[m, top : top + tile, lanes[0]], res[m, top : top + tile, lanes[1]]
            d, b = res[m, top + rows : top + rows + tile, lanes[0]], res[m, top + rows : top + rows + tile, lanes[1]]
            g.append((a - b, c + d))
            h.append((a + b, d - c))
        values = {}
        for parts, plain, turned, sign in ((g, 0, 1, 1), (h, 2, 3, -1)):
            (r0, i0), (r1, i1), (r2, i2), (r3, i3) = parts
            if plain in outs:
                values[plain] = (r0 + r2) + (r1 + r3), (i0 + i2) + (i1 + i3)
            if turned in outs:
                ro, io = r1 - r3, i1 - i3
                if sign > 0:
                    values[turned] = (r0 - r2) + io, (i0 - i2) - ro
                else:
                    values[turned] = (r0 - r2) - io, (i0 - i2) + ro
        return values

    def add_terms(res, h, outs):
        for k in range(steps // 2):
            for r in range(0, chd, 2 * tile):
                halves = []
                for r8 in (r, r + tile):
                    sums = {}
                    for w in range(wd):
                        values = lag_values(res, 2 * k * rows + w * chd + r8, outs)
                        for out in outs:
                            re, im = values[out]
                            inv = lax.rsqrt(jnp.maximum(re * re + im * im, phase_floor * phase_floor))
                            for q, value in enumerate((re, re * inv, im * inv)):
                                sums[out, q] = value if w == 0 else sums[out, q] + value
                    halves.append(sums)
                for out in outs:
                    for q in range(3):
                        first = ((h * (steps // 2) + k) * 3 + q) * chd + r
                        value = jnp.concatenate([half[out, q] for half in halves], axis=0)
                        ts[first : first + 2 * tile, out * CHUNK : (out + 1) * CHUNK] = value.astype(bf16)

    both_res = (res_a, res_b)
    part_rows = steps * rows

    def correlate(table, h):
        for m in range(4):
            both_res[h][m] = dot(xs[h * part_rows : (h + 1) * part_rows, m * 256 : (m + 1) * 256], table[m])

    for h in range(2):
        correlate(edge_ref, h)
        add_terms(both_res[h], h, (2, 3))
    oe[...] = dot(wmat[...], ts[:, 2 * CHUNK :])

    def bin_sums(u, m, h):
        add_terms(both_res[h], h, (0, 1, 2, 3))
        if h == 0:
            return
        part = p1.shape[3:]
        value = dot(wmat[...], ts[...])
        lane = lax.broadcasted_iota(jnp.int32, (wmat.shape[0], CHUNK), 1)
        for out, w in enumerate((nwin // 2 + m, m, nwin // 2 - 1 - m, nwin - 1 - m)):
            piece_out = value[:, out * CHUNK : (out + 1) * CHUNK]
            if out >= 2:
                at = (out - 2) * CHUNK + m
                piece_out = jnp.where((lane + u) == 0, oe[:, at : at + 1], piece_out)
            p1[u, w % 2, w // 2] = piece_out.reshape(part).astype(bf16)

    def copy1(u):
        return remote(p1.at[u, 1 - w1], r1.at[u], s1.at[u], q1.at[u], dev1())

    def copy2(u, k):
        return remote(
            b2.at[u, lax.rem(w2 + k, g2)], r2.at[u, k - 1], s2.at[u, k - 1], q2.at[u, k - 1], dev2(k)
        )

    def copy3(u):
        return remote(b3.at[u, 1 - c1], r3.at[u], s3.at[u], q3.at[u], dev3())

    def copy4(u, k):
        return remote(
            b4.at[u, lax.rem(c2 + k, g4)], r4.at[u, k - 1], s4.at[u, k - 1], q4.at[u, k - 1], dev4(k)
        )

    def copy2_odd(u, k):
        return remote(
            b2o.at[u, lax.rem(w2 + k, g2)], r2o.at[u, k - 1], s2.at[u, k - 1], q2.at[u, k - 1], dev2(k)
        )

    def copy3_odd(u):
        return remote(b3o.at[u, 1 - c1], r3o.at[u], s3.at[u], q3.at[u], dev3())

    def by_parity(u, even, odd):
        pl.when(lax.rem(u, 2) == 0)(lambda: even(u))
        pl.when(lax.rem(u, 2) == 1)(lambda: odd(u))

    def stage2_even(u):
        for i in range(g2):
            b2[u, i] = (p1[u, w1, i].astype(f32) + r1[u, i].astype(f32)).astype(bf16)
        for k in range(1, g2):
            copy2(u, k).start()
        a2[u] = p1[u, w1, w2].astype(f32) + r1[u, w2].astype(f32)

    def stage2_odd(u):
        for i in range(g2):
            for c in range(2):
                b3o[u, c, i] = (p1[u, w1, i, c].astype(f32) + r1[u, i, c].astype(f32)).astype(bf16)
        copy3_odd(u).start()
        for i in range(g2):
            a3o[u, i] = p1[u, w1, i, c1].astype(f32) + r1[u, i, c1].astype(f32)

    def stage2(u):
        copy1(u).wait()
        by_parity(u, stage2_even, stage2_odd)

    def stage3_even(u):
        for k in range(1, g2):
            copy2(u, k).wait()
        for i in range(2):
            total = a2[u, i]
            for k in range(1, g2):
                total = total + r2[u, k - 1, i].astype(f32)
            a3[u, i] = total
            b3[u, i] = total.astype(bf16)
        copy3(u).start()

    def stage3_odd(u):
        copy3_odd(u).wait()
        for i in range(g2):
            total = a3o[u, i] + r3o[u, i].astype(f32)
            a3o[u, i] = total
            b2o[u, i] = total.astype(bf16)
        for k in range(1, g2):
            copy2_odd(u, k).start()

    def stage3(u):
        by_parity(u, stage3_even, stage3_odd)

    def stage4_even(u):
        copy3(u).wait()
        for i in range(g4):
            total = a3[u, c1, i] + r3[u, i].astype(f32)
            a4[u, i] = total
            b4[u, i] = total.astype(bf16)

    def stage4_odd(u):
        for k in range(1, g2):
            copy2_odd(u, k).wait()
        for i in range(g4):
            total = a3o[u, w2, i]
            for k in range(1, g2):
                total = total + r2o[u, k - 1, i].astype(f32)
            a4[u, i] = total
            b4[u, i] = total.astype(bf16)

    def stage4(u):
        by_parity(u, stage4_even, stage4_odd)
        for k in range(1, g4):
            copy4(u, k).start()

    def stage5(u):
        for k in range(1, g4):
            copy4(u, k).wait()
        total = a4[u, c2]
        for k in range(1, g4):
            total = total + r4[u, k - 1].astype(f32)
        n = total.shape[0] // 3
        lin, pr, pi = total[:n], total[n : 2 * n], total[2 * n :]
        count = traces[:n, :]
        fin[u] = lin * lax.rsqrt(count) * ((pr * pr + pi * pi) / count)

    jobs = [(m, h) for m in range(blocks) for h in range(2)]
    table_copy(0).wait()
    for n, (m, h) in enumerate(jobs):
        correlate(tab.at[0, m], h)
        if n:
            bin_sums(0, *jobs[n - 1])

    def turn(v, carry):
        @pl.when(v < units)
        def _():
            table_copy(v).wait()
            for n, (m, h) in enumerate(jobs):
                correlate(tab.at[v, m], h)
                if n:
                    bin_sums(v, *jobs[n - 1])
                else:
                    bin_sums(v - 1, *jobs[-1])
                    copy1(v - 1).start()

        @pl.when(v == units)
        def _():
            bin_sums(v - 1, *jobs[-1])
            copy1(v - 1).start()

        for stage, lag in ((stage2, 1), (stage3, 3), (stage4, 5), (stage5, 7)):
            @pl.when((v >= lag) & (v < units + lag))
            def _(stage=stage, lag=lag):
                stage(v - lag)

        return carry

    lax.fori_loop(1, units + 7, turn, 0)

    ri = lax.broadcasted_iota(jnp.int32, (CHUNK, CHUNK), 0)
    rj = lax.broadcasted_iota(jnp.int32, (CHUNK, CHUNK), 1)
    flip = jnp.where(ri + rj == CHUNK, 1.0, 0.0).astype(bf16)
    lane = lax.broadcasted_iota(jnp.int32, fin.shape[1:], 1)
    for u in range(units):
        value = fin[units - 1 - u]
        hi = value.astype(bf16)
        rest = value - hi.astype(f32)
        mid = rest.astype(bf16)
        low = (rest - mid.astype(f32)).astype(bf16)
        value = dot(hi, flip) + dot(mid, flip) + dot(low, flip)
        value = jnp.where(lane == 0, fin[(units - u) % units], value)
        value = jnp.where((lane * 0 + me_w // blocks) % 2 == 1, value, fin[u])
        o_ref[:, u * CHUNK : (u + 1) * CHUNK] = value


def shards(spectra, sources, bin_rows):
    chd, wd = spectra.shape[0], spectra.shape[1]
    steps = sources.shape[0]
    nchan, nwin = lax.axis_size("chan"), lax.axis_size("win")
    lag_dev = LAGS // nwin
    units, blocks = lag_dev // CHUNK, nwin // 4
    bl = NBINS // nchan
    rows = wd * chd
    g2, g4 = nwin // 2, nchan // 2
    x = jnp.transpose(spectra, (2, 1, 0, 3)).reshape(2, rows, F)

    table, edge = lag_tables(lag_dev)
    per = NBINS * 3 * steps // nchan
    piece = 2 * F // nchan
    tail = (per, CHUNK)
    cfg = (nchan, nwin, steps, wd, chd, units, blocks)
    dma = pltpu.SemaphoreType.DMA
    vmem = pl.BlockSpec(memory_space=pltpu.VMEM)
    slots = jnp.transpose(bin_rows[:, 0], (0, 2, 1))
    out = pl.pallas_call(
        functools.partial(kernel, cfg),
        out_shape=jax.ShapeDtypeStruct((steps * bl, lag_dev), f32),
        in_specs=[vmem, pl.BlockSpec(memory_space=pltpu.SMEM), vmem, vmem] + [pl.BlockSpec(memory_space=pl.ANY)],
        out_specs=vmem,
        scratch_shapes=[
            pltpu.VMEM((units, blocks, 4, F // 4, 2 * CHUNK), bf16),
            pltpu.VMEM((nchan, steps * wd, piece + 128), bf16),
            pltpu.VMEM((nchan - 1, steps * wd, piece + 128), bf16),
            pltpu.VMEM((nchan, steps * wd, piece), bf16),
            pltpu.VMEM((rows, F), bf16),
            pltpu.VMEM((rows, F), bf16),
            pltpu.VMEM((steps * wd, F), f32),
            pltpu.VMEM((steps * wd, F), f32),
            pltpu.VMEM((steps * 2 * rows, F), bf16),
            pltpu.VMEM((NBINS * 3 * steps, 3 * steps * chd), bf16),
            pltpu.VMEM((3 * steps * chd, 4 * CHUNK), bf16),
            pltpu.VMEM((NBINS * 3 * steps, 2 * CHUNK), f32),
            pltpu.VMEM((steps * wd, 128), f32),
            pltpu.VMEM((units, steps * bl, CHUNK), f32),
            pltpu.VMEM((4, steps * rows, 2 * CHUNK), f32),
            pltpu.VMEM((4, steps * rows, 2 * CHUNK), f32),
            pltpu.VMEM((units, 2, g2, 2, g4) + tail, bf16),
            pltpu.VMEM((units, g2, 2, g4) + tail, bf16),
            pltpu.VMEM((units, 2, g4) + tail, f32),
            pltpu.VMEM((units, g2, 2, g4) + tail, bf16),
            pltpu.VMEM((units, g2 - 1, 2, g4) + tail, bf16),
            pltpu.VMEM((units, 2, g4) + tail, f32),
            pltpu.VMEM((units, 2, g4) + tail, bf16),
            pltpu.VMEM((units, g4) + tail, bf16),
            pltpu.VMEM((units, g4) + tail, f32),
            pltpu.VMEM((units, g4) + tail, bf16),
            pltpu.VMEM((units, g4 - 1) + tail, bf16),
            pltpu.VMEM((units, g2, g4) + tail, f32),
            pltpu.VMEM((units, 2, g2, g4) + tail, bf16),
            pltpu.VMEM((units, g2, g4) + tail, bf16),
            pltpu.VMEM((units, g2, g4) + tail, bf16),
            pltpu.VMEM((units, g2 - 1, g4) + tail, bf16),
            dma((units,)),
            dma((nchan - 1,)), dma((nchan - 1,)), dma((nchan - 1,)), dma((nchan - 1,)),
            dma((units,)), dma((units,)),
            dma((units, g2 - 1)), dma((units, g2 - 1)),
            dma((units,)), dma((units,)),
            dma((units, g4 - 1)), dma((units, g4 - 1)),
        ],
        compiler_params=pltpu.CompilerParams(
            collective_id=0, has_side_effects=True, vmem_limit_bytes=56 * 1024 * 1024
        ),
        name="stack",
    )(x, sources, slots, jnp.asarray(edge), jnp.asarray(table))
    return out.reshape(steps, bl, lag_dev)


def solution(mesh):
    in_specs = (P("chan", "win", None, None), P(), P(None, "chan", None, None))
    out_specs = P(None, "chan", "win")
    return jax.shard_map(shards, mesh=mesh, in_specs=in_specs, out_specs=out_specs, check_vma=False)
```

```python
import functools

import jax
import jax.numpy as jnp
import ml_dtypes
import numpy as np
from jax import lax
from jax.experimental import pallas as pl
from jax.experimental.pallas import tpu as pltpu
from jax.sharding import PartitionSpec as P

F = 1024
F0 = 32
NFFT = 8192
LMAX = 2048
HW = 32
NBINS = 32
MOST = 3
LAGS = 4096
CHUNK = 128

epsilon_amp = 1e-06
phase_floor = 0.1

f32 = jnp.float32
bf16 = jnp.bfloat16
MESH = pl.DeviceIdType.MESH


def lag_tables(lag_dev):
    blocks = LMAX // 2 // lag_dev
    units = lag_dev // CHUNK
    freq = F0 + np.arange(F, dtype=np.int64)

    def trig(lags):
        turn = (freq[:, None] * lags[None, :]) % NFFT
        angle = turn * (2.0 * np.pi / NFFT)
        both = np.zeros((F, 256), np.float32)
        both[:, : lags.size] = np.cos(angle).astype(ml_dtypes.bfloat16)
        both[:, CHUNK : CHUNK + lags.size] = np.sin(angle).astype(ml_dtypes.bfloat16)
        both = (both * F ** -0.5).astype(ml_dtypes.bfloat16)
        return np.stack([both[m::4] for m in range(4)])

    starts = [[m * lag_dev + u * CHUNK for m in range(blocks)] for u in range(units)]
    table = np.stack([np.stack([trig(t + np.arange(CHUNK)) for t in at]) for at in starts])
    return table, trig((np.arange(blocks) + 1) * lag_dev)


def dot(a, b):
    return jnp.dot(a, b, preferred_element_type=f32)


def smooth_band(amp, band):
    hi = amp.astype(bf16)
    lo = (amp - hi.astype(f32)).astype(bf16)
    count = F // 256
    parts = []
    for j in range(count):
        first, last = max(j - 1, 0), min(j + 2, count)
        piece = band[(first - j + 1) * 256 : (last - j + 1) * 256, :]
        cols = slice(first * 256, last * 256)
        parts.append(dot(hi[:, cols], piece) + dot(lo[:, cols], piece))
    return jnp.concatenate(parts, axis=1) * (1.0 / (2 * HW + 1)) + epsilon_amp


def whiten(re, im, band):
    inv = 1.0 / smooth_band(jnp.sqrt(re * re + im * im), band)
    return (re * inv).astype(bf16), (im * inv).astype(bf16)


def kernel(
    cfg,
    x_ref, sources_ref, bins_ref, edge_ref, tab_hbm,
    o_ref,
    tab, sbuf, rsr, ag, wr_s, wi_s, sr_s, si_s, xs, wmat, ts, oe, traces, fin, res_a, res_b,
    p1, r1, a2, b2, r2, a3, b3, r3, a4, b4, r4, a3o, b3o, r3o, b2o, r2o,
    tab_sem, rs_s, rs_r, ag_s, ag_r, s1, q1, s2, q2, s3, q3, s4, q4,
):
    nchan, nwin, steps, wd, chd, units, blocks = cfg
    g2, g4 = nwin // 2, nchan // 2
    rows = wd * chd
    me_c, me_w = lax.axis_index("chan"), lax.axis_index("win")
    w1, w2 = lax.rem(me_w, 2), me_w // 2
    c1, c2 = lax.rem(me_c, 2), me_c // 2

    def chan_dev(k):
        return (lax.rem(me_c + k, nchan), me_w)

    def dev1():
        return (me_c, me_w + 1 - 2 * w1)

    def dev2(k):
        return (me_c, lax.rem(w2 + k, g2) * 2 + w1)

    def dev3():
        return (me_c + 1 - 2 * c1, me_w)

    def dev4(k):
        return (lax.rem(c2 + k, g4) * 2 + c1, me_w)

    def table_copy(u):
        return pltpu.make_async_copy(tab_hbm.at[u], tab.at[u], tab_sem.at[u])

    def remote(src, dst, s, r, dev):
        return pltpu.make_async_remote_copy(
            src_ref=src, dst_ref=dst, send_sem=s, recv_sem=r, device_id=dev, device_id_type=MESH
        )

    for u in range(units):
        table_copy(u).start()

    barrier = pltpu.get_barrier_semaphore()
    partners = [chan_dev(k) for k in range(1, nchan)] + [dev1()] + [dev2(k) for k in range(1, g2)]
    for dev in partners:
        pl.semaphore_signal(barrier, inc=1, device_id=dev, device_id_type=MESH)

    piece = 2 * F // nchan
    bl = NBINS // nchan
    row = lax.broadcasted_iota(jnp.int32, (steps * wd, rows), 0)
    col = lax.broadcasted_iota(jnp.int32, (steps * wd, rows), 1)
    want = jnp.full(row.shape, -1, jnp.int32)
    for s in range(steps):
        loc = sources_ref[s] - me_c * chd
        loc = jnp.where((loc >= 0) & (loc < chd), loc, -wd * chd - 1)
        want = jnp.where(row // wd == s, (row % wd) * chd + loc, want)
    pick = jnp.where(col == want, 1.0, 0.0).astype(bf16)
    both = jnp.concatenate([dot(pick, x_ref[0]), dot(pick, x_ref[1])], axis=1).astype(bf16)
    slots = [bins_ref[s].astype(f32) for s in range(steps)]

    def bins_of(shape, dims):
        i = lax.broadcasted_iota(jnp.int32, shape, len(shape) - 2)
        b = sum(lax.broadcasted_iota(jnp.int32, shape, d) * size for d, size in dims) * bl + i % bl
        hit = lax.broadcasted_iota(jnp.int32, shape, len(shape) - 1) == b
        return jnp.where(hit, 1.0, 0.0).reshape(-1, NBINS).astype(bf16), (i // bl).reshape(-1, NBINS)[:, 0:1]

    def pick_slots(chosen, values):
        return lax.dot_general(chosen, values, (((1,), (1,)), ((), ())), preferred_element_type=f32)

    chosen, step = bins_of((nchan, steps * bl, NBINS), [(0, 1)])
    cnt = jnp.zeros(step.shape, f32)
    for s in range(steps):
        live = pick_slots(chosen, jnp.where(slots[s] >= 0.0, 1.0, 0.0).astype(bf16))
        cnt = jnp.where(step == s, jnp.sum(live, axis=1, keepdims=True), cnt)
    cnt = jnp.broadcast_to(cnt, (nchan * steps * bl, 128)).astype(bf16)
    for d in range(nchan):
        sbuf[d, :, :piece] = both[:, d * piece : (d + 1) * piece]
        sbuf[d, :, piece:] = jnp.zeros((steps * wd, 128), bf16)
        sbuf[d, : steps * bl, piece:] = cnt[d * steps * bl : (d + 1) * steps * bl]
    pl.semaphore_wait(barrier, len(partners))

    def rs_copy(k):
        return remote(
            sbuf.at[lax.rem(me_c + k, nchan)], rsr.at[k - 1], rs_s.at[k - 1], rs_r.at[k - 1], chan_dev(k)
        )

    def ag_copy(k):
        return remote(ag.at[me_c], ag.at[me_c], ag_s.at[k - 1], ag_r.at[k - 1], chan_dev(k))

    for k in range(1, nchan):
        rs_copy(k).start()

    bi = lax.broadcasted_iota(jnp.int32, (768, 256), 0)
    bj = lax.broadcasted_iota(jnp.int32, (768, 256), 1)
    band = jnp.where(jnp.abs(bi - 256 - bj) <= HW, 1.0, 0.0).astype(bf16)
    wr, wi = whiten(x_ref[0].astype(f32), x_ref[1].astype(f32), band)
    pi_ = lax.broadcasted_iota(jnp.int32, (F, F), 0)
    pj = lax.broadcasted_iota(jnp.int32, (F, F), 1)
    order = jnp.where(pi_ == (pj & 255) * 4 + (pj >> 8), 1.0, 0.0).astype(bf16)
    wr_s[...] = dot(wr, order).astype(bf16)
    wi_s[...] = dot(wi, order).astype(bf16)

    for k in range(1, nchan):
        rs_copy(k).wait()
    total = sbuf[me_c].astype(f32)
    for k in range(1, nchan):
        total = total + rsr[k - 1].astype(f32)
    ag[me_c] = total[:, :piece].astype(bf16)
    traces[...] = jnp.maximum(total[:, piece:], 1.0) * (wd * nwin)
    for k in range(1, nchan):
        ag_copy(k).start()

    shape = (2, g4, 3, steps * bl, NBINS)
    chosen, step = bins_of(shape, [(0, 1), (1, 2)])
    term = lax.broadcasted_iota(jnp.int32, shape, 2).reshape(-1, NBINS)[:, 0:1]
    offset = ((step * 3 + term) * chd).astype(f32)
    slots_at = pick_slots(chosen, slots[0].astype(bf16))
    for s in range(1, steps):
        slots_at = jnp.where(step == s, pick_slots(chosen, slots[s].astype(bf16)), slots_at)
    slots_at = jnp.where(slots_at >= 0.0, slots_at + offset, -1.0)
    wcol = lax.broadcasted_iota(jnp.int32, wmat.shape, 1).astype(f32)
    hit = wcol < 0.0
    for k in range(MOST):
        hit = hit | (wcol == slots_at[:, k : k + 1])
    wmat[...] = jnp.where(hit, 1.0, 0.0).astype(bf16)

    for k in range(1, nchan):
        ag_copy(k).wait()
    half = nchan // 2
    sre = jnp.concatenate([ag[d] for d in range(half)], axis=1).astype(f32)
    sim = jnp.concatenate([ag[d] for d in range(half, nchan)], axis=1).astype(f32)
    sr, si = whiten(sre, sim, band)
    sr_s[...] = dot(sr, order)
    si_s[...] = dot(si, order)

    for w in range(wd):
        here = slice(w * chd, (w + 1) * chd)
        wrw = wr_s[here, :].astype(f32)
        wiw = wi_s[here, :].astype(f32)
        for s in range(steps):
            i = s * wd + w
            a, b = sr_s[i : i + 1, :], si_s[i : i + 1, :]
            first = 2 * s * rows + w * chd
            xs[first : first + chd, :] = (wrw * a + wiw * b).astype(bf16)
            xs[first + rows : first + rows + chd, :] = (wiw * a - wrw * b).astype(bf16)

    tile = 8
    lanes = (slice(0, CHUNK), slice(CHUNK, 2 * CHUNK))

    def lag_values(res, top, outs):
        g, h = [], []
        for m in range(4):
            a, c = res[m, top : top + tile, lanes[0]], res[m, top : top + tile, lanes[1]]
            d, b = res[m, top + rows : top + rows + tile, lanes[0]], res[m, top + rows : top + rows + tile, lanes[1]]
            g.append((a - b, c + d))
            h.append((a + b, d - c))
        values = {}
        for parts, plain, turned, sign in ((g, 0, 1, 1), (h, 2, 3, -1)):
            (r0, i0), (r1, i1), (r2, i2), (r3, i3) = parts
            if plain in outs:
                values[plain] = (r0 + r2) + (r1 + r3), (i0 + i2) + (i1 + i3)
            if turned in outs:
                ro, io = r1 - r3, i1 - i3
                if sign > 0:
                    values[turned] = (r0 - r2) + io, (i0 - i2) - ro
                else:
                    values[turned] = (r0 - r2) - io, (i0 - i2) + ro
        return values

    def add_terms(res, h, outs):
        for k in range(steps // 2):
            for r in range(0, chd, 2 * tile):
                halves = []
                for r8 in (r, r + tile):
                    sums = {}
                    for w in range(wd):
                        values = lag_values(res, 2 * k * rows + w * chd + r8, outs)
                        for out in outs:
                            re, im = values[out]
                            inv = lax.rsqrt(jnp.maximum(re * re + im * im, phase_floor * phase_floor))
                            for q, value in enumerate((re, re * inv, im * inv)):
                                sums[out, q] = value if w == 0 else sums[out, q] + value
                    halves.append(sums)
                for out in outs:
                    for q in range(3):
                        first = ((h * (steps // 2) + k) * 3 + q) * chd + r
                        value = jnp.concatenate([half[out, q] for half in halves], axis=0)
                        ts[first : first + 2 * tile, out * CHUNK : (out + 1) * CHUNK] = value.astype(bf16)

    both_res = (res_a, res_b)
    part_rows = steps * rows

    def correlate(table, h):
        for m in range(4):
            both_res[h][m] = dot(xs[h * part_rows : (h + 1) * part_rows, m * 256 : (m + 1) * 256], table[m])

    for h in range(2):
        correlate(edge_ref, h)
        add_terms(both_res[h], h, (2, 3))
    oe[...] = dot(wmat[...], ts[:, 2 * CHUNK :])

    def bin_sums(u, m, h):
        add_terms(both_res[h], h, (0, 1, 2, 3))
        if h == 0:
            return
        part = p1.shape[3:]
        value = dot(wmat[...], ts[...])
        lane = lax.broadcasted_iota(jnp.int32, (wmat.shape[0], CHUNK), 1)
        for out, w in enumerate((nwin // 2 + m, m, nwin // 2 - 1 - m, nwin - 1 - m)):
            piece_out = value[:, out * CHUNK : (out + 1) * CHUNK]
            if out >= 2:
                at = (out - 2) * CHUNK + m
                piece_out = jnp.where((lane + u) == 0, oe[:, at : at + 1], piece_out)
            p1[u, w % 2, w // 2] = piece_out.reshape(part).astype(bf16)

    def copy1(u):
        return remote(p1.at[u, 1 - w1], r1.at[u], s1.at[u], q1.at[u], dev1())

    def copy2(u, k):
        return remote(
            b2.at[u, lax.rem(w2 + k, g2)], r2.at[u, k - 1], s2.at[u, k - 1], q2.at[u, k - 1], dev2(k)
        )

    def copy3(u):
        return remote(b3.at[u, 1 - c1], r3.at[u], s3.at[u], q3.at[u], dev3())

    def copy4(u, k):
        return remote(
            b4.at[u, lax.rem(c2 + k, g4)], r4.at[u, k - 1], s4.at[u, k - 1], q4.at[u, k - 1], dev4(k)
        )

    def copy2_odd(u, k):
        return remote(
            b2o.at[u, lax.rem(w2 + k, g2)], r2o.at[u, k - 1], s2.at[u, k - 1], q2.at[u, k - 1], dev2(k)
        )

    def copy3_odd(u):
        return remote(b3o.at[u, 1 - c1], r3o.at[u], s3.at[u], q3.at[u], dev3())

    def by_parity(u, even, odd):
        pl.when(lax.rem(u, 2) == 0)(lambda: even(u))
        pl.when(lax.rem(u, 2) == 1)(lambda: odd(u))

    def stage2_even(u):
        for i in range(g2):
            b2[u, i] = (p1[u, w1, i].astype(f32) + r1[u, i].astype(f32)).astype(bf16)
        for k in range(1, g2):
            copy2(u, k).start()
        a2[u] = p1[u, w1, w2].astype(f32) + r1[u, w2].astype(f32)

    def stage2_odd(u):
        for i in range(g2):
            for c in range(2):
                b3o[u, c, i] = (p1[u, w1, i, c].astype(f32) + r1[u, i, c].astype(f32)).astype(bf16)
        copy3_odd(u).start()
        for i in range(g2):
            a3o[u, i] = p1[u, w1, i, c1].astype(f32) + r1[u, i, c1].astype(f32)

    def stage2(u):
        copy1(u).wait()
        by_parity(u, stage2_even, stage2_odd)

    def stage3_even(u):
        for k in range(1, g2):
            copy2(u, k).wait()
        for i in range(2):
            total = a2[u, i]
            for k in range(1, g2):
                total = total + r2[u, k - 1, i].astype(f32)
            a3[u, i] = total
            b3[u, i] = total.astype(bf16)
        copy3(u).start()

    def stage3_odd(u):
        copy3_odd(u).wait()
        for i in range(g2):
            total = a3o[u, i] + r3o[u, i].astype(f32)
            a3o[u, i] = total
            b2o[u, i] = total.astype(bf16)
        for k in range(1, g2):
            copy2_odd(u, k).start()

    def stage3(u):
        by_parity(u, stage3_even, stage3_odd)

    def stage4_even(u):
        copy3(u).wait()
        for i in range(g4):
            total = a3[u, c1, i] + r3[u, i].astype(f32)
            a4[u, i] = total
            b4[u, i] = total.astype(bf16)

    def stage4_odd(u):
        for k in range(1, g2):
            copy2_odd(u, k).wait()
        for i in range(g4):
            total = a3o[u, w2, i]
            for k in range(1, g2):
                total = total + r2o[u, k - 1, i].astype(f32)
            a4[u, i] = total
            b4[u, i] = total.astype(bf16)

    def stage4(u):
        by_parity(u, stage4_even, stage4_odd)
        for k in range(1, g4):
            copy4(u, k).start()

    def stage5(u):
        for k in range(1, g4):
            copy4(u, k).wait()
        total = a4[u, c2]
        for k in range(1, g4):
            total = total + r4[u, k - 1].astype(f32)
        n = total.shape[0] // 3
        lin, pr, pi = total[:n], total[n : 2 * n], total[2 * n :]
        count = traces[:n, :]
        fin[u] = lin * lax.rsqrt(count) * ((pr * pr + pi * pi) / count)

    jobs = [(m, h) for m in range(blocks) for h in range(2)]
    table_copy(0).wait()
    for n, (m, h) in enumerate(jobs):
        correlate(tab.at[0, m], h)
        if n:
            bin_sums(0, *jobs[n - 1])

    def turn(v, carry):
        @pl.when(v < units)
        def _():
            table_copy(v).wait()
            for n, (m, h) in enumerate(jobs):
                correlate(tab.at[v, m], h)
                if n:
                    bin_sums(v, *jobs[n - 1])
                else:
                    bin_sums(v - 1, *jobs[-1])
                    copy1(v - 1).start()

        @pl.when(v == units)
        def _():
            bin_sums(v - 1, *jobs[-1])
            copy1(v - 1).start()

        for stage, lag in ((stage5, 7), (stage4, 5), (stage3, 3), (stage2, 1)):
            @pl.when((v >= lag) & (v < units + lag))
            def _(stage=stage, lag=lag):
                stage(v - lag)

        return carry

    lax.fori_loop(1, units + 7, turn, 0)

    ri = lax.broadcasted_iota(jnp.int32, (CHUNK, CHUNK), 0)
    rj = lax.broadcasted_iota(jnp.int32, (CHUNK, CHUNK), 1)
    flip = jnp.where(ri + rj == CHUNK, 1.0, 0.0).astype(bf16)
    lane = lax.broadcasted_iota(jnp.int32, fin.shape[1:], 1)
    for u in range(units):
        value = fin[units - 1 - u]
        hi = value.astype(bf16)
        rest = value - hi.astype(f32)
        mid = rest.astype(bf16)
        low = (rest - mid.astype(f32)).astype(bf16)
        value = dot(hi, flip) + dot(mid, flip) + dot(low, flip)
        value = jnp.where(lane == 0, fin[(units - u) % units], value)
        value = jnp.where((lane * 0 + me_w // blocks) % 2 == 1, value, fin[u])
        o_ref[:, u * CHUNK : (u + 1) * CHUNK] = value


def shards(spectra, sources, bin_rows):
    chd, wd = spectra.shape[0], spectra.shape[1]
    steps = sources.shape[0]
    nchan, nwin = lax.axis_size("chan"), lax.axis_size("win")
    lag_dev = LAGS // nwin
    units, blocks = lag_dev // CHUNK, nwin // 4
    bl = NBINS // nchan
    rows = wd * chd
    g2, g4 = nwin // 2, nchan // 2
    x = jnp.transpose(spectra, (2, 1, 0, 3)).reshape(2, rows, F)

    table, edge = lag_tables(lag_dev)
    per = NBINS * 3 * steps // nchan
    piece = 2 * F // nchan
    tail = (per, CHUNK)
    cfg = (nchan, nwin, steps, wd, chd, units, blocks)
    dma = pltpu.SemaphoreType.DMA
    vmem = pl.BlockSpec(memory_space=pltpu.VMEM)
    slots = jnp.transpose(bin_rows[:, 0], (0, 2, 1))
    out = pl.pallas_call(
        functools.partial(kernel, cfg),
        out_shape=jax.ShapeDtypeStruct((steps * bl, lag_dev), f32),
        in_specs=[vmem, pl.BlockSpec(memory_space=pltpu.SMEM), vmem, vmem] + [pl.BlockSpec(memory_space=pl.ANY)],
        out_specs=vmem,
        scratch_shapes=[
            pltpu.VMEM((units, blocks, 4, F // 4, 2 * CHUNK), bf16),
            pltpu.VMEM((nchan, steps * wd, piece + 128), bf16),
            pltpu.VMEM((nchan - 1, steps * wd, piece + 128), bf16),
            pltpu.VMEM((nchan, steps * wd, piece), bf16),
            pltpu.VMEM((rows, F), bf16),
            pltpu.VMEM((rows, F), bf16),
            pltpu.VMEM((steps * wd, F), f32),
            pltpu.VMEM((steps * wd, F), f32),
            pltpu.VMEM((steps * 2 * rows, F), bf16),
            pltpu.VMEM((NBINS * 3 * steps, 3 * steps * chd), bf16),
            pltpu.VMEM((3 * steps * chd, 4 * CHUNK), bf16),
            pltpu.VMEM((NBINS * 3 * steps, 2 * CHUNK), f32),
            pltpu.VMEM((steps * wd, 128), f32),
            pltpu.VMEM((units, steps * bl, CHUNK), f32),
            pltpu.VMEM((4, steps * rows, 2 * CHUNK), f32),
            pltpu.VMEM((4, steps * rows, 2 * CHUNK), f32),
            pltpu.VMEM((units, 2, g2, 2, g4) + tail, bf16),
            pltpu.VMEM((units, g2, 2, g4) + tail, bf16),
            pltpu.VMEM((units, 2, g4) + tail, f32),
            pltpu.VMEM((units, g2, 2, g4) + tail, bf16),
            pltpu.VMEM((units, g2 - 1, 2, g4) + tail, bf16),
            pltpu.VMEM((units, 2, g4) + tail, f32),
            pltpu.VMEM((units, 2, g4) + tail, bf16),
            pltpu.VMEM((units, g4) + tail, bf16),
            pltpu.VMEM((units, g4) + tail, f32),
            pltpu.VMEM((units, g4) + tail, bf16),
            pltpu.VMEM((units, g4 - 1) + tail, bf16),
            pltpu.VMEM((units, g2, g4) + tail, f32),
            pltpu.VMEM((units, 2, g2, g4) + tail, bf16),
            pltpu.VMEM((units, g2, g4) + tail, bf16),
            pltpu.VMEM((units, g2, g4) + tail, bf16),
            pltpu.VMEM((units, g2 - 1, g4) + tail, bf16),
            dma((units,)),
            dma((nchan - 1,)), dma((nchan - 1,)), dma((nchan - 1,)), dma((nchan - 1,)),
            dma((units,)), dma((units,)),
            dma((units, g2 - 1)), dma((units, g2 - 1)),
            dma((units,)), dma((units,)),
            dma((units, g4 - 1)), dma((units, g4 - 1)),
        ],
        compiler_params=pltpu.CompilerParams(
            collective_id=0, has_side_effects=True, vmem_limit_bytes=56 * 1024 * 1024
        ),
        name="stack",
    )(x, sources, slots, jnp.asarray(edge), jnp.asarray(table))
    return out.reshape(steps, bl, lag_dev)


def solution(mesh):
    in_specs = (P("chan", "win", None, None), P(), P(None, "chan", None, None))
    out_specs = P(None, "chan", "win")
    return jax.shard_map(shards, mesh=mesh, in_specs=in_specs, out_specs=out_specs, check_vma=False)
```
